512 devices in a mesh: resp: 32 (over z, x_hi, core), ctx: 16 (over y, x_lo).
Axes of the slice: x: 4 (x_hi: 2, x_lo: 2; x = x_hi * 2 + x_lo), y: 8, z: 8, core: 2. Of those that a mesh axis runs over, the one named last changes fastest.
Arguments:
- query: bfloat16 [32, 2048, 1024], P('resp', 'ctx'), may hold values from -8 to 8
- resp_key: bfloat16 [32, 2048, 128], P('resp', 'ctx'), may hold values from -6 to 6
- resp_value: bfloat16 [32, 2048, 128], P('resp', 'ctx'), may hold values from -6 to 6
- prompt_key: bfloat16 [2048, 128], P('resp'), may hold values from -8 to 8
- prompt_value: bfloat16 [2048, 128], P('resp'), may hold values from -6 to 6
- saved_out: bfloat16 [32, 2048, 1024], P('resp', 'ctx'), may hold values from -6 to 6
- out_grad: bfloat16 [32, 2048, 1024], P('resp', 'ctx'), may hold values from -6 to 6
- resp_len: int32 [32], P('resp'), may hold values from 512 to 2048, as said below
- prompt_order: int32 [32], replicated, may hold values from 0 to 31, each once
Outputs:
- dquery: bfloat16 [32, 2048, 1024], P('resp', 'ctx')
- resp_dkey: bfloat16 [32, 2048, 128], P('resp', 'ctx')
- resp_dvalue: bfloat16 [32, 2048, 128], P('resp', 'ctx')
- prompt_dkey: bfloat16 [2048, 128], P('resp')
- prompt_dvalue: bfloat16 [2048, 128], P('resp')
The draws below stay inside these ranges and needn't reach their ends.
Inputs may be any that keep to these rules, and one draw needn't show every extreme that they name: A permutation: block j of the stored prompt rows sits at block prompt_order[j] of the prompt. `resp_len`: at least a quarter of each response is not padding; some response has all 2048 tokens.
All inputs are finite; a program needn't handle non-finite values.
Results may differ from the reference program's by a relative error of at most 0.0051.
Values may be sent and summed in bfloat16 or wider, within the bound.
A program may use at most 64 MiB of HBM per device.

```python
import jax
import jax.numpy as jnp
from jax import lax

HEADS = 8
HEAD_DIM = 128
PROMPT_DEV = 64
RESPONSES = 32
PROMPT_BLOCKS = 32
RESP_LEN = 2048
PROMPT = 2048


def draw_prompt_key(key, part):
    key = jax.random.fold_in(key, 11)
    values_drawn = jnp.clip(jax.random.normal(key, (PROMPT, HEAD_DIM), jnp.float32), -6.0, 6.0)
    return values_drawn.astype(jnp.bfloat16)


def draw_query(key, part):
    key = jax.random.fold_in(key, 12)
    array_shape = (RESPONSES, RESP_LEN, HEADS * HEAD_DIM)
    values_drawn = jnp.clip(jax.random.normal(key, array_shape, jnp.float32), -6.0, 6.0)
    return values_drawn.astype(jnp.bfloat16)


def draw_resp_len(key, part):
    key = jax.random.fold_in(key, 13)
    lengths = jax.random.randint(key, (RESPONSES,), RESP_LEN // 4, RESP_LEN + 1)
    longest = jax.random.randint(jax.random.fold_in(key, 1), (), 0, RESPONSES)
    return jnp.where(jnp.arange(RESPONSES) == longest, RESP_LEN, lengths).astype(jnp.int32)


def level_of(stream_key, shape, cuts, low, largest):
    loudness = 1.0
    for axis_at, parts in cuts:
        draws = jax.random.uniform(jax.random.fold_in(jax.random.fold_in(stream_key, 6), axis_at), (parts,), jnp.float32, low / len(cuts), largest / len(cuts))
        loudness = loudness * jnp.repeat(jnp.exp(draws), shape[axis_at] // parts).reshape((-1,) + (1,) * (len(shape) - 1 - axis_at))
    return loudness


def centred(own_key, dims, width, most, pieces=(), kind=jnp.bfloat16):
    values = width * jax.random.normal(own_key, dims, jnp.float32)
    if pieces:
        values = values * level_of(own_key, dims, pieces, -0.22, 0.18)
    return jnp.clip(values, -most, most).astype(kind)


def setup_inputs(seed: int = 0) -> dict:
    keys = jax.random.split(jax.random.key(seed), 10)
    return {
        "query": draw_query(jax.random.fold_in(keys[9], 71), 0),
        "resp_key": centred(keys[1], (RESPONSES, RESP_LEN, HEAD_DIM), 1.0, 6.0, ((0, 32), (1, 16))),
        "resp_value": centred(keys[2], (RESPONSES, RESP_LEN, HEAD_DIM), 1.0, 6.0, ((0, 32), (1, 16))),
        "prompt_key": draw_prompt_key(jax.random.fold_in(keys[9], 71), 0),
        "prompt_value": centred(keys[4], (PROMPT, HEAD_DIM), 1.0, 6.0, ((0, 32),)),
        "saved_out": centred(keys[5], (RESPONSES, RESP_LEN, HEADS * HEAD_DIM), 1.0, 6.0, ((0, 32), (1, 16))),
        "out_grad": centred(keys[6], (RESPONSES, RESP_LEN, HEADS * HEAD_DIM), 1.0, 6.0, ((0, 32), (1, 16))),
        "resp_len": draw_resp_len(jax.random.fold_in(keys[9], 71), 0),
        "prompt_order": jax.random.permutation(keys[8], PROMPT_BLOCKS).astype(jnp.int32),
    }


mask_floor = -1e30


def scores_of(queries, key_rows, score_scale):
    return jnp.einsum("thd,kd->thk", queries.astype(jnp.float32), key_rows.astype(jnp.float32), precision=lax.Precision.HIGHEST) * score_scale


def half_round(values):
    return lax.optimization_barrier(values.astype(jnp.bfloat16)).astype(jnp.float32)


def tile_grads(queries, grads_out, log_norm, row_delta, key_rows, value_rows, allowed, score_scale):
    scores = scores_of(queries, key_rows, score_scale)
    probs = jnp.where(allowed, jnp.exp(scores - log_norm[..., None]), 0.0)
    dprobs = jnp.einsum("thd,kd->thk", grads_out.astype(jnp.float32), value_rows.astype(jnp.float32), precision=lax.Precision.HIGHEST)
    dscores = probs * (dprobs - row_delta[..., None]) * score_scale
    probs_half = half_round(probs)
    dscores_half = half_round(dscores)
    dquery_tile = jnp.einsum("thk,kd->thd", dscores_half, key_rows.astype(jnp.float32), precision=lax.Precision.HIGHEST)
    dkey_tile = jnp.einsum("thk,thd->kd", dscores_half, queries.astype(jnp.float32), precision=lax.Precision.HIGHEST)
    dvalue_tile = jnp.einsum("thk,thd->kd", probs_half, grads_out.astype(jnp.float32), precision=lax.Precision.HIGHEST)
    return dquery_tile, dkey_tile, dvalue_tile


def reference(query, resp_key, resp_value, prompt_key, prompt_value, saved_out, out_grad, resp_len, prompt_order):
    score_scale = HEAD_DIM ** -0.5
    positions = jnp.arange(RESP_LEN, dtype=jnp.int32)
    causal = (positions[None, :] <= positions[:, None])[:, None, :]

    def one_response(prompt_sums, inputs):
        query_rows, resp_keys, resp_values, saved_rows, grad_rows, resp_length = inputs
        queries = query_rows.reshape(RESP_LEN, HEADS, HEAD_DIM).transpose(1, 0, 2)[:, :, None, :]
        grads_all = grad_rows.reshape(RESP_LEN, HEADS, HEAD_DIM).transpose(1, 0, 2)[:, :, None, :]
        saved_all = saved_rows.reshape(RESP_LEN, HEADS, HEAD_DIM).transpose(1, 0, 2)[:, :, None, :]
        live_rows = (positions < resp_length)[:, None, None]

        def head_grads(head_inputs):
            head_queries, head_grads_out, head_saved = head_inputs
            row_delta = jnp.sum(head_grads_out.astype(jnp.float32) * head_saved.astype(jnp.float32), axis=-1)
            prompt_scores = scores_of(head_queries, prompt_key, score_scale)
            resp_scores = jnp.where(causal, scores_of(head_queries, resp_keys, score_scale), mask_floor)
            row_max = jnp.maximum(jnp.max(prompt_scores, axis=-1), jnp.max(resp_scores, axis=-1))
            row_sum = jnp.sum(jnp.exp(prompt_scores - row_max[..., None]), axis=-1)
            row_sum = row_sum + jnp.sum(jnp.where(causal, jnp.exp(resp_scores - row_max[..., None]), 0.0), axis=-1)
            log_norm = row_max + jnp.log(row_sum)
            prompt_part = tile_grads(head_queries, head_grads_out, log_norm, row_delta, prompt_key, prompt_value, live_rows, score_scale)
            resp_part = tile_grads(head_queries, head_grads_out, log_norm, row_delta, resp_keys, resp_values, live_rows & causal, score_scale)
            return (prompt_part[0] + resp_part[0], prompt_part[1], prompt_part[2], resp_part[1], resp_part[2])

        head_results = lax.map(head_grads, (queries, grads_all, saved_all))
        dquery_rows = head_results[0][:, :, 0, :].transpose(1, 0, 2).reshape(RESP_LEN, HEADS * HEAD_DIM).astype(jnp.bfloat16)
        prompt_sums = (prompt_sums[0] + jnp.sum(head_results[1], axis=0), prompt_sums[1] + jnp.sum(head_results[2], axis=0))
        dkey_rows = jnp.sum(head_results[3], axis=0).astype(jnp.bfloat16)
        dvalue_rows = jnp.sum(head_results[4], axis=0).astype(jnp.bfloat16)
        return prompt_sums, (dquery_rows, dkey_rows, dvalue_rows)

    start_sums = (jnp.zeros((PROMPT, HEAD_DIM), jnp.float32), jnp.zeros((PROMPT, HEAD_DIM), jnp.float32))
    prompt_sums, outputs = lax.scan(one_response, start_sums, (query, resp_key, resp_value, saved_out, out_grad, resp_len))
    dquery, resp_dkey, resp_dvalue = outputs
    inverse = jnp.argsort(prompt_order)
    prompt_dkey = prompt_sums[0].reshape(PROMPT_BLOCKS, PROMPT_DEV, HEAD_DIM)[inverse].reshape(PROMPT, HEAD_DIM).astype(jnp.bfloat16)
    prompt_dvalue = prompt_sums[1].reshape(PROMPT_BLOCKS, PROMPT_DEV, HEAD_DIM)[inverse].reshape(PROMPT, HEAD_DIM).astype(jnp.bfloat16)
    return (dquery, resp_dkey, resp_dvalue, prompt_dkey, prompt_dvalue)
```

```python
import math

import jax
import jax.numpy as jnp
from jax import lax
from jax.experimental import pallas as pl
from jax.experimental.pallas import tpu as pltpu
from jax.sharding import PartitionSpec as P

MESH = pl.DeviceIdType.MESH
HEADS = 8
DIM = 128
SCALE = DIM ** (-0.5)
SCALE2 = SCALE * math.log2(math.e)
FLOOR = -1e30
RING = 8
HALF = RING // 2
GROUP = 16
PB = 64
RB = 128
CHUNK = 256
TOKENS = 128
ROWS = TOKENS * HEADS
COLS = ROWS
VMEM = 56 * 1024 * 1024
F32 = jnp.float32
BF16 = jnp.bfloat16


def level_at(s, idx):
    k = (s + 1) // 2
    odd = lax.rem(s, 2)
    return lax.rem(idx + RING + k - 2 * k * odd, RING)


def body(
    q_ref, rk_ref, rv_ref, pk_ref, pv_ref, o_ref, do_ref, len_ref, ord_ref,
    dq_ref, rdk_ref, rdv_ref, pdk_ref, pdv_ref,
    pkv, rkv, qs, dos, qt, dot, delta, pst, gst, mst, m_run, l_run, fac, dqt, inv,
    c1_own, c1_send, c1_recv, c2_send, c2_recv,
    rs_send, rs_recv, ag_send, ag_recv,
    d_own, d_send, d_recv, d_tot, d_xsend, d_xrecv,
    a_rs, a_zs, a_cs, a_xs, b_rs, b_ys, b_xs,
    c1_ss, c1_rs, c2_ss, c2_rs, rs_ss, rs_rs, ag_ss, ag_rs,
    d_ss, d_rs, dx_ss, dx_rs, token,
):
    resp = lax.axis_index("resp")
    ctx = lax.axis_index("ctx")
    z, xh, core = resp // 4, lax.rem(resp // 2, 2), lax.rem(resp, 2)
    y, xl = ctx // 2, lax.rem(ctx, 2)
    z_low = resp - z * 4

    def at_z(step):
        return (lax.rem(z + RING + step, RING) * 4 + z_low, ctx)

    def at_y(step):
        return (resp, lax.rem(y + RING + step, RING) * 2 + xl)

    other_core = (resp + 1 - 2 * core, ctx)
    mirror = (resp + 2 - 4 * xh, ctx + 1 - 2 * xl)
    x_pair = (resp, ctx + 1 - 2 * xl)

    def at_ctx(step):
        return (resp, lax.rem(ctx + step, GROUP))

    def remote(src, dst, ss, rs, device):
        return pltpu.make_async_remote_copy(
            src_ref=src, dst_ref=dst, send_sem=ss, recv_sem=rs,
            device_id=device, device_id_type=MESH,
        )

    barrier = pltpu.get_barrier_semaphore()
    partners = [at_z(1), at_z(-1), at_y(1), at_y(-1), other_core, mirror, x_pair]
    for device in partners:
        pl.semaphore_signal(barrier, inc=1, device_id=device, device_id_type=MESH)

    own_p = resp
    pkv[pl.ds(pl.multiple_of(own_p * PB, PB), PB), 0:DIM] = pk_ref[...]
    pkv[pl.ds(pl.multiple_of(own_p * PB, PB), PB), DIM:] = pv_ref[...]
    rkv[pl.ds(pl.multiple_of(ctx * RB, RB), RB), 0:DIM] = rk_ref[...]
    rkv[pl.ds(pl.multiple_of(ctx * RB, RB), RB), DIM:] = rv_ref[...]
    pl.semaphore_wait(barrier, len(partners))

    def p_block(lev, sub, c):
        return lev * 4 + sub * 2 + c

    def p_slot(b):
        return pkv.at[pl.ds(pl.multiple_of(b * PB, PB), PB)]

    def r_slot(b):
        return rkv.at[pl.ds(pl.multiple_of(b * RB, RB), RB)]

    def a_block(s, own):
        return p_block(level_at(s, z), xh if own else 1 - xh, core)

    def b_block(s, own):
        return level_at(s, y) * 2 + (xl if own else 1 - xl)

    ring_a = (p_slot, a_block, a_rs, a_zs, at_z)
    ring_b = (r_slot, b_block, b_rs, b_ys, at_y)

    def ring_copy(ring, s, own, up):
        slot, block, rs, ss, at = ring
        b = block(s, own)
        return remote(
            slot(b), slot(b), ss.at[s, (0 if own else 2) + (0 if up else 1)], rs.at[b],
            at(1 if up else -1),
        )

    def arrived(ring, b):
        slot, _, rs, ss, at = ring
        remote(slot(b), slot(b), ss.at[0, 0], rs.at[b], at(1)).wait_recv()

    def core_copy(s, own):
        b = a_block(s, own)
        return remote(p_slot(b), p_slot(b), a_cs.at[s, 0 if own else 1], a_rs.at[b], other_core)

    def hops(ring, s, own, act):
        if isinstance(s, int):
            assert s == 0
            act(ring_copy(ring, s, own, True))
            act(ring_copy(ring, s, own, False))
            return
        k = (s + 1) // 2
        odd = lax.rem(s, 2) == 1
        up_limit, down_limit = (HALF, HALF - 1) if own else (HALF - 1, HALF)

        @pl.when(odd & (k < up_limit))
        def _():
            act(ring_copy(ring, s, own, True))

        @pl.when(jnp.logical_not(odd) & (k < down_limit))
        def _():
            act(ring_copy(ring, s, own, False))

    start = lambda copy: copy.start()
    sent = lambda copy: copy.wait_send()

    def ring_step(ring, s, core_too):
        for own in (True, False):
            arrived(ring, ring[1](s, own))
            hops(ring, s, own, start)
            if core_too:
                core_copy(s, own).start()

    a_first = a_block(0, True)
    b_first = b_block(0, True)
    a_mirror = remote(p_slot(a_first), p_slot(a_first), a_xs, a_rs.at[a_first], mirror)
    b_pair = remote(r_slot(b_first), r_slot(b_first), b_xs, b_rs.at[b_first], x_pair)
    a_mirror.start()
    b_pair.start()
    hops(ring_a, 0, True, start)
    hops(ring_b, 0, True, start)
    core_copy(0, True).start()

    for h in range(HEADS):
        lanes = slice(h * DIM, (h + 1) * DIM)
        q = q_ref[:, lanes]
        do = do_ref[:, lanes]
        qs[lanes, :] = q
        dos[lanes, :] = do
        qt[:, lanes] = q.T
        do_t = do.astype(F32).T
        dot[:, lanes] = do_t.astype(BF16)
        delta[:, lanes] = jnp.sum(do_t * o_ref[:, lanes].astype(F32).T, axis=0, keepdims=True)

    m_run[...] = jnp.full_like(m_run, FLOOR)
    l_run[...] = jnp.zeros_like(l_run)
    dqt[...] = jnp.zeros_like(dqt)

    def inverse_of(c, _):
        at = jnp.int32(0)
        for j in range(RING * 4):
            at = jnp.maximum(at, j * (ord_ref[j] == c).astype(jnp.int32))
        inv[c] = at
        return 0

    lax.fori_loop(0, RING * 4, inverse_of, 0)

    arrived(ring_a, a_block(0, False))
    hops(ring_a, 0, False, start)
    core_copy(0, False).start()
    arrived(ring_b, b_block(0, False))
    hops(ring_b, 0, False, start)

    def first_pass(kv, lev, chunk, causal):
        rows = pl.ds(pl.multiple_of(lev * CHUNK, CHUNK), CHUNK)
        blocks = pl.ds(chunk * 4, 4)
        keys = kv[rows, 0:DIM]
        values = kv[rows, DIM:]
        keys_t = keys.T
        for ct in range(ROWS // COLS):
            cols = slice(ct * COLS, (ct + 1) * COLS)
            s = jnp.dot(keys, qt[:, cols], preferred_element_type=F32) * SCALE2
            if causal:
                key_pos = lev * CHUNK + lax.broadcasted_iota(jnp.int32, (CHUNK, COLS), 0)
                lane = lax.broadcasted_iota(jnp.int32, (CHUNK, COLS), 1)
                query_pos = ctx * TOKENS + (lane & (TOKENS - 1))
                s = jnp.where(key_pos <= query_pos, s, FLOOR)
            m_old = m_run[:, cols]
            m_new = jnp.maximum(m_old, jnp.max(s, axis=0, keepdims=True))
            alpha = jnp.exp2(m_old - m_new)
            p = jnp.exp2(s - m_new)
            l_run[:, cols] = l_run[:, cols] * alpha + jnp.sum(p, axis=0, keepdims=True)
            dp = jnp.dot(values, dot[:, cols], preferred_element_type=F32)
            g = (p * (dp - delta[:, cols])).astype(BF16)
            pst[blocks, :, cols] = p.astype(BF16).reshape(4, PB, COLS)
            gst[blocks, :, cols] = g.reshape(4, PB, COLS)
            dq = jnp.dot(keys_t, g, preferred_element_type=F32)
            dqt[:, cols] = dqt[:, cols] * alpha + dq
            m_run[:, cols] = m_new
            mst[chunk, :, cols] = m_new

    def first(s, _):
        @pl.when(s >= 1)
        def _():
            ring_step(ring_a, s, True)

        lev = level_at(s, z)
        arrived(ring_a, p_block(lev, 0, 1 - core))
        arrived(ring_a, p_block(lev, 1, 1 - core))
        first_pass(pkv, lev, lev, False)

        @pl.when(s >= 1)
        def _():
            ring_step(ring_b, s, False)

        r_lev = level_at(s, y)

        @pl.when(r_lev <= y)
        def _():
            first_pass(rkv, r_lev, RING + r_lev, True)

        return 0

    lax.fori_loop(0, RING, first, 0)
    pl.semaphore_signal(token, inc=1, device_id=mirror, device_id_type=MESH)

    lane = lax.broadcasted_iota(jnp.int32, (1, ROWS), 1)
    live = ctx * TOKENS + (lane & (TOKENS - 1)) < len_ref[0]
    m_all = m_run[...]
    inv_l = jnp.where(live, 1.0 / l_run[...], 0.0)
    for i in range(2 * RING):
        factor = jnp.exp2(mst[i] - m_all) * inv_l
        for b in range(4):
            fac[4 * i + b] = factor

    def scaled(store, block):
        return (store[block].astype(F32) * fac[block]).astype(BF16)

    def c1_copy(lev):
        return remote(c1_send.at[lev], c1_recv.at[lev], c1_ss.at[lev], c1_rs.at[lev], other_core)

    def c_term(lev, sub):
        return c1_own[lev, sub] + c1_recv[lev, sub]

    routes = ((4, 2, True, ()), (3, 1, True, ()), (3, 2, False, ()), (2, 2, True, (0, 1)),
              (2, 1, False, ()), (1, 1, True, ()), (1, 1, False, (2, 4)))

    def c_copy(m, up):
        d = 0 if up else 1
        go = routes[m][1]
        return remote(c2_send.at[d, m], c2_recv.at[d, m], c2_ss.at[d, m], c2_rs.at[d, m], at_z(go if up else -go))

    def c_message(m, up):
        d = 0 if up else 1
        dist, _, longer, added = routes[m]
        value = c_term(lax.rem(z + RING + (dist if up else -dist), RING), d if longer else 1 - d)
        for a in added:
            c_copy(a, up).wait_recv()
            value = value + c2_recv[d, a].astype(F32)
        c2_send[d, m] = value.astype(BF16)
        c_copy(m, up).start()

    def c_events(s):
        if s == 6:
            c1_copy(lax.rem(z + HALF, RING)).wait_recv()
            c_message(0, True)
            c_message(0, False)
        plain = {5: (3, True), 4: (3, False), 3: (2, True), 2: (2, False), 1: (1, True), 0: (1, False)}
        if s in plain:
            dist, up = plain[s]
            c1_copy(lax.rem(z + RING + (dist if up else -dist), RING)).wait_recv()
            for m in {3: (1, 2), 2: (4,), 1: (5,)}[dist]:
                c_message(m, up)
        if s == 1:
            c_message(3, True)
            c_message(3, False)
        if s == 0:
            c_message(6, True)
            c_message(6, False)

    def c_total(sub):
        d = sub
        value = c_term(z, sub)
        for m, up in ((3, d == 0), (5, d == 0), (6, d == 1)):
            value = value + c2_recv[0 if up else 1, m].astype(F32)
        return value

    def d_copy(j, kv, up):
        d = 0 if up else 1
        at = at_y(1 if up else -1)
        if j == 1:
            return remote(d_send.at[d, 0, kv, d], d_recv.at[d, 0, kv, d], d_ss.at[d, 0, kv], d_rs.at[d, 0, kv], at)
        return remote(d_send.at[d, j - 1, kv], d_recv.at[d, j - 1, kv], d_ss.at[d, j - 1, kv], d_rs.at[d, j - 1, kv], at)

    def d_step(j):
        dist = HALF + 1 - j
        for kv in range(2):
            for up in (True, False):
                d = 0 if up else 1
                if j > 1:
                    d_copy(j - 1, kv, up).wait_recv()
                lev = lax.rem(y + RING + (dist if up else -dist), RING)
                for sub in range(2):
                    begins = sub == d
                    if j == 1 and not begins:
                        continue
                    value = d_own[lev, kv, sub]
                    if j > 2 or (j == 2 and begins):
                        value = value + d_recv[d, j - 2, kv, sub].astype(F32)
                    d_send[d, j - 1, kv, sub] = value.astype(BF16)
                d_copy(j, kv, up).start()

    def second(i, _):
        s = RING - 1 - i
        lev = level_at(s, z)
        ps, gs = [], []
        for b in range(4):
            stored = inv[lev * 4 + b]
            ps.append(scaled(pst, stored))
            gs.append(scaled(gst, stored))
        dv = jnp.dot(jnp.concatenate(ps, axis=0), dos[...], preferred_element_type=F32)
        dk = jnp.dot(jnp.concatenate(gs, axis=0), qs[...], preferred_element_type=F32) * SCALE
        for sub in range(2):
            for c in range(2):
                rows = slice((sub * 2 + c) * PB, (sub * 2 + c + 1) * PB)

                @pl.when(core == c)
                def _():
                    c1_own[lev, sub, :, 0:DIM] = dk[rows]
                    c1_own[lev, sub, :, DIM:] = dv[rows]

                @pl.when(core != c)
                def _():
                    c1_send[lev, sub, :, 0:DIM] = dk[rows]
                    c1_send[lev, sub, :, DIM:] = dv[rows]

        c1_copy(lev).start()

        r_lev = level_at(s, y)

        @pl.when(r_lev <= y)
        def _():
            first = (RING + r_lev) * 4
            ps = jnp.concatenate([scaled(pst, first + b) for b in range(4)], axis=0)
            gs = jnp.concatenate([scaled(gst, first + b) for b in range(4)], axis=0)
            dv = jnp.dot(ps, dos[...], preferred_element_type=F32)
            dk = jnp.dot(gs, qs[...], preferred_element_type=F32) * SCALE
            for sub in range(2):
                rows = slice(sub * RB, (sub + 1) * RB)
                d_own[r_lev, 0, sub] = dk[rows]
                d_own[r_lev, 1, sub] = dv[rows]

        @pl.when(r_lev > y)
        def _():
            d_own[r_lev] = jnp.zeros((2, 2, RB, DIM), F32)

        for when in range(RING - 1):

            @pl.when(s == when)
            def _():
                c_events(when)

        for j, when in ((1, 7), (2, 3)):

            @pl.when(s == when)
            def _():
                d_step(j)

        return 0

    lax.fori_loop(0, RING, second, 0)

    inv_scaled = inv_l * SCALE
    for h in range(HEADS):
        lanes = slice(h * DIM, (h + 1) * DIM)
        dq_ref[:, lanes] = (dqt[:, lanes] * inv_scaled[:, lanes]).T.astype(BF16)

    d_step(3)

    c1_copy(z).wait_recv()
    for up in (True, False):
        for m in (3, 5, 6):
            c_copy(m, up).wait_recv()
    for sub in range(2):
        value = c_total(sub)
        for i in range(GROUP):
            r, c = i // 2, i % 2
            rs_send[sub, i] = value[r * 8 : (r + 1) * 8, c * DIM : (c + 1) * DIM]

    def rs_copy(dx, step):
        to_xh = xh if dx == 0 else 1 - xh
        to_ctx = lax.rem(ctx + step, GROUP)
        return remote(
            rs_send.at[to_xh, to_ctx], rs_recv.at[dx, step], rs_ss.at[dx, step], rs_rs.at[dx, step],
            (z * 4 + to_xh * 2 + core, to_ctx),
        )

    def ag_copy(step):
        return remote(ag_send, ag_recv.at[ctx], ag_ss.at[step], ag_rs.at[step], at_ctx(step))

    pieces = [(dx, step) for step in range(GROUP) for dx in range(2)][1:]
    pl.semaphore_wait(token, 1)
    for dx, step in pieces:
        rs_copy(dx, step).start()

    d_step(4)

    piece = rs_send[xh, ctx]
    for dx, step in pieces:
        rs_copy(dx, step).wait_recv()
        piece = piece + rs_recv[dx, step]
    ag_send[...] = piece
    ag_recv[ctx] = piece
    for step in range(1, GROUP):
        ag_copy(step).start()

    for kv in range(2):
        for up in (True, False):
            d_copy(HALF, kv, up).wait_recv()
        for sub in range(2):
            d_tot[kv, sub] = d_own[y, kv, sub] + sum(d_recv[d, HALF - 1, kv, sub].astype(F32) for d in range(2))
        d_xsend[kv] = d_tot[kv, 1 - xl].astype(BF16)

    def dx_copy(kv):
        return remote(d_xsend.at[kv], d_xrecv.at[kv], dx_ss.at[kv], dx_rs.at[kv], x_pair)

    for kv in range(2):
        dx_copy(kv).start()
    for kv, out in ((0, rdk_ref), (1, rdv_ref)):
        dx_copy(kv).wait_recv()
        out[...] = (d_tot[kv, xl] + d_xrecv[kv].astype(F32)).astype(BF16)

    for step in range(1, GROUP):
        ag_copy(step).wait_recv()
    for c, out in ((0, pdk_ref), (1, pdv_ref)):
        parts = [ag_recv[2 * r + c] for r in range(GROUP // 2)]
        out[...] = jnp.concatenate(parts, axis=0).astype(BF16)

    a_mirror.wait_send()
    b_pair.wait_send()
    for kv in range(2):
        dx_copy(kv).wait_send()
    for dx, step in pieces:
        rs_copy(dx, step).wait_send()
    for step in range(1, GROUP):
        ag_copy(step).wait_send()
    for up in (True, False):
        for m in range(len(routes)):
            c_copy(m, up).wait_send()
        for j in range(1, HALF + 1):
            for kv in range(2):
                d_copy(j, kv, up).wait_send()
    for own in (True, False):
        hops(ring_a, 0, own, sent)
        hops(ring_b, 0, own, sent)
        core_copy(0, own).wait_send()

    def drain(s, _):
        for own in (True, False):
            hops(ring_a, s, own, sent)
            hops(ring_b, s, own, sent)
            core_copy(s, own).wait_send()
        return 0

    lax.fori_loop(1, RING, drain, 0)

    def drain_c1(s, _):
        c1_copy(s).wait_send()
        return 0

    lax.fori_loop(0, RING, drain_c1, 0)


def hand_over(*refs):
    n = (len(refs) - 1) // 2
    copies = [pltpu.make_async_copy(refs[i], refs[n + i], refs[-1].at[i]) for i in range(n)]
    for copy in copies:
        copy.start()
    for copy in copies:
        copy.wait()


def local(query, resp_key, resp_value, prompt_key, prompt_value, saved_out, out_grad, resp_len, prompt_order):
    vmem = pl.BlockSpec(memory_space=pltpu.VMEM)
    smem = pl.BlockSpec(memory_space=pltpu.SMEM)
    dma = pltpu.SemaphoreType.DMA
    wide = 2 * DIM
    outs = pl.pallas_call(
        body,
        out_shape=(
            jax.ShapeDtypeStruct((TOKENS, HEADS * DIM), BF16),
            jax.ShapeDtypeStruct((RB, DIM), BF16),
            jax.ShapeDtypeStruct((RB, DIM), BF16),
            jax.ShapeDtypeStruct((PB, DIM), BF16),
            jax.ShapeDtypeStruct((PB, DIM), BF16),
        ),
        in_specs=[vmem] * 7 + [smem] * 2,
        out_specs=(vmem,) * 5,
        scratch_shapes=[
            pltpu.VMEM((RING * CHUNK, wide), BF16),
            pltpu.VMEM((RING * CHUNK, wide), BF16),
            pltpu.VMEM((ROWS, DIM), BF16),
            pltpu.VMEM((ROWS, DIM), BF16),
            pltpu.VMEM((DIM, ROWS), BF16),
            pltpu.VMEM((DIM, ROWS), BF16),
            pltpu.VMEM((1, ROWS), F32),
            pltpu.VMEM((2 * RING * 4, PB, ROWS), BF16),
            pltpu.VMEM((2 * RING * 4, PB, ROWS), BF16),
            pltpu.VMEM((2 * RING, 1, ROWS), F32),
            pltpu.VMEM((1, ROWS), F32),
            pltpu.VMEM((1, ROWS), F32),
            pltpu.VMEM((2 * RING * 4, 1, ROWS), F32),
            pltpu.VMEM((DIM, ROWS), F32),
            pltpu.SMEM((RING * 4,), jnp.int32),
            pltpu.VMEM((RING, 2, PB, wide), F32),
            pltpu.VMEM((RING, 2, PB, wide), F32),
            pltpu.VMEM((RING, 2, PB, wide), F32),
            pltpu.VMEM((2, 7, PB, wide), BF16),
            pltpu.VMEM((2, 7, PB, wide), BF16),
            pltpu.VMEM((2, GROUP, 8, DIM), F32),
            pltpu.VMEM((2, GROUP, 8, DIM), F32),
            pltpu.VMEM((8, DIM), F32),
            pltpu.VMEM((GROUP, 8, DIM), F32),
            pltpu.VMEM((RING, 2, 2, RB, DIM), F32),
            pltpu.VMEM((2, HALF, 2, 2, RB, DIM), BF16),
            pltpu.VMEM((2, HALF, 2, 2, RB, DIM), BF16),
            pltpu.VMEM((2, 2, RB, DIM), F32),
            pltpu.VMEM((2, RB, DIM), BF16),
            pltpu.VMEM((2, RB, DIM), BF16),
            dma((RING * 4,)),
            dma((RING, 4)),
            dma((RING, 2)),
            dma,
            dma((GROUP,)),
            dma((RING, 4)),
            dma,
            dma((RING,)),
            dma((RING,)),
            dma((2, 7)),
            dma((2, 7)),
            dma((2, GROUP)),
            dma((2, GROUP)),
            dma((GROUP,)),
            dma((GROUP,)),
            dma((2, HALF, 2)),
            dma((2, HALF, 2)),
            dma((2,)),
            dma((2,)),
            pltpu.SemaphoreType.REGULAR,
        ],
        compiler_params=pltpu.CompilerParams(
            collective_id=0, has_side_effects=True, vmem_limit_bytes=VMEM
        ),
        name="attention_backward",
    )(
        query[0], resp_key[0], resp_value[0], prompt_key, prompt_value,
        saved_out[0], out_grad[0], resp_len, prompt_order,
    )
    anywhere = pl.BlockSpec(memory_space=pl.ANY)
    outs = pl.pallas_call(
        hand_over,
        out_shape=tuple(jax.ShapeDtypeStruct(out.shape, out.dtype) for out in outs),
        in_specs=[anywhere] * 5,
        out_specs=(anywhere,) * 5,
        scratch_shapes=[dma((5,))],
        compiler_params=pltpu.CompilerParams(vmem_limit_bytes=VMEM),
        name="hand_over",
    )(*outs)
    return (outs[0][None], outs[1][None], outs[2][None], outs[3], outs[4])


def solution(mesh):
    token = P("resp", "ctx", None)
    block = P("resp", None)
    return jax.shard_map(
        local,
        mesh=mesh,
        in_specs=(token, token, token, block, block, token, token, P("resp"), P()),
        out_specs=(token, token, token, block, block),
        check_vma=False,
    )
```

```python
import math

import jax
import jax.numpy as jnp
from jax import lax
from jax.experimental import pallas as pl
from jax.experimental.pallas import tpu as pltpu
from jax.sharding import PartitionSpec as P

MESH = pl.DeviceIdType.MESH
HEADS = 8
DIM = 128
SCALE = DIM ** (-0.5)
SCALE2 = SCALE * math.log2(math.e)
FLOOR = -1e30
RING = 8
HALF = RING // 2
GROUP = 16
PB = 64
RB = 128
CHUNK = 256
TOKENS = 128
ROWS = TOKENS * HEADS
VMEM = 56 * 1024 * 1024
F32 = jnp.float32
BF16 = jnp.bfloat16


def level_at(s, idx):
    k = (s + 1) // 2
    odd = lax.rem(s, 2)
    return lax.rem(idx + RING + k - 2 * k * odd, RING)


def body(
    q_hbm, rk_hbm, rv_hbm, pk_hbm, pv_hbm, o_hbm, do_hbm, len_ref, order_ref,
    dq_ref, rdk_ref, rdv_ref, pdk_ref, pdv_ref,
    q_ref, o_ref, do_ref, pkv, rkeys, rvalues, qs, dos, qt, dot, delta, pst, gst, mst, m_run, m_dq, l_run, fac, dqt, dqr, inv_v, inv,
    c1_own, c1_send, c1_recv, c2_send, c2_recv,
    rs_send, rs_recv, ag_recv,
    d_own, d_send, d_recv, d_tot, d_xsend, d_xrecv,
    in_s, inv_s, a_rs, a_cr, a_ss, bk_rs, bk_ss, bv_rs, bv_ss,
    c1_ss, c1_rs, c2_ss, c2_rs, rs_ss, rs_rs, ag_ss, ag_rs,
    d_ss, d_rs, dx_ss, dx_rs, token,
):
    resp = lax.axis_index("resp")
    ctx = lax.axis_index("ctx")
    z, xh, core = resp // 4, lax.rem(resp // 2, 2), lax.rem(resp, 2)
    y, xl = ctx // 2, lax.rem(ctx, 2)
    z_low = resp - z * 4

    def at_z(step, across=False):
        low, c = (z_low + 2 - 4 * xh, ctx + 1 - 2 * xl) if across else (z_low, ctx)
        return (lax.rem(z + RING + step, RING) * 4 + low, c)

    def at_y(step, across=False):
        return (resp, lax.rem(y + RING + step, RING) * 2 + (1 - xl if across else xl))

    other_core = (resp + 1 - 2 * core, ctx)
    mirror = (resp + 2 - 4 * xh, ctx + 1 - 2 * xl)
    x_pair = (resp, ctx + 1 - 2 * xl)

    def at_ctx(step):
        return (resp, lax.rem(ctx + step, GROUP))

    def remote(src, dst, ss, rs, device):
        return pltpu.make_async_remote_copy(
            src_ref=src, dst_ref=dst, send_sem=ss, recv_sem=rs,
            device_id=device, device_id_type=MESH,
        )

    barrier = pltpu.get_barrier_semaphore()
    partners = [other_core, mirror, x_pair]
    partners += [at(step, across) for at in (at_z, at_y) for step in (1, -1) for across in (False, True)]
    for device in partners:
        pl.semaphore_signal(barrier, inc=1, device_id=device, device_id_type=MESH)

    p_rows = pl.ds(pl.multiple_of(resp * PB, PB), PB)
    r_rows = pl.ds(pl.multiple_of(ctx * RB, RB), RB)
    moves = (
        (pk_hbm, pkv.at[p_rows, 0:DIM]), (pv_hbm, pkv.at[p_rows, DIM : 2 * DIM]),
        (rk_hbm, rkeys.at[r_rows]), (rv_hbm, rvalues.at[r_rows]),
        (q_hbm, q_ref), (do_hbm, do_ref), (o_hbm, o_ref),
    )
    reads = [pltpu.make_async_copy(src, dst, in_s.at[i]) for i, (src, dst) in enumerate(moves)]
    for read in reads:
        read.start()
    for read in reads[:4]:
        read.wait()
    pl.semaphore_wait(barrier, len(partners))

    def p_block(lev, sub, c):
        return lev * 4 + sub * 2 + c

    def p_slot(b):
        return pkv.at[pl.ds(pl.multiple_of(b * PB, PB), PB)]

    def r_slot(buffer):
        return lambda b: buffer.at[pl.ds(pl.multiple_of(b * RB, RB), RB)]

    def a_block(s, own):
        return p_block(level_at(s, z), xh if own else 1 - xh, core)

    def b_block(s, own):
        return level_at(s, y) * 2 + (xl if own else 1 - xl)

    ring_a = (p_slot, a_block, lambda b: a_rs.at[b // 2], a_ss, at_z)
    ring_k = (r_slot(rkeys), b_block, lambda b: bk_rs.at[b], bk_ss, at_y)
    ring_v = (r_slot(rvalues), b_block, lambda b: bv_rs.at[b], bv_ss, at_y)

    def ring_copy(ring, s, own, device):
        slot, block, rs, ss, _ = ring
        b = block(s, own)
        return remote(slot(b), slot(b), ss, rs(b), device)

    def arrived(ring, b):
        slot, _, rs, ss, at = ring
        remote(slot(b), slot(b), ss, rs(b), at(1)).wait_recv()

    def core_copy(s, own):
        b = a_block(s, own)
        return remote(p_slot(b), p_slot(b), a_ss, a_cr.at[b // 4], other_core)

    def core_arrived(lev):
        both = pkv.at[pl.ds(pl.multiple_of(lev * CHUNK, CHUNK), 2 * PB)]
        remote(both, both, a_ss, a_cr.at[lev], other_core).wait_recv()

    def all_sent(ref, ss):
        remote(ref, ref, ss, dx_rs.at[0], other_core).wait_send()

    def hops(ring, s, own):
        k = (s + 1) // 2
        odd = lax.rem(s, 2) == 1
        up_limit, down_limit = (HALF, HALF - 1) if own else (HALF - 1, HALF)

        @pl.when(odd & (k < up_limit))
        def _():
            ring_copy(ring, s, own, ring[4](1)).start()

        @pl.when(jnp.logical_not(odd) & (k < down_limit))
        def _():
            ring_copy(ring, s, own, ring[4](-1)).start()

    def ring_step(ring, s, core_too):
        for own in (True, False):
            arrived(ring, ring[1](s, own))
            hops(ring, s, own)
            if core_too:
                core_copy(s, own).start()

    def first_copies(ring, pair):
        for step in (1, -1):
            for across in (False, True):
                ring_copy(ring, 0, True, ring[4](step, across)).start()
        ring_copy(ring, 0, True, pair).start()

    first_copies(ring_a, mirror)
    core_copy(0, True).start()
    first_copies(ring_k, x_pair)
    first_copies(ring_v, x_pair)

    def prepare(h):
        lanes = slice(h * DIM, (h + 1) * DIM)
        q = q_ref[:, lanes]
        do = do_ref[:, lanes]
        qs[lanes, :] = q
        dos[lanes, :] = do
        qt[:, lanes] = q.T
        dot[:, lanes] = do.T
        product = do.astype(F32) * o_ref[:, lanes].astype(F32)
        delta[:, lanes] = jnp.sum(product.T, axis=0, keepdims=True)

    for read in reads[4:]:
        read.wait()
    for h in range(HEADS):
        prepare(h)
    arrived(ring_a, a_block(0, False))
    core_copy(0, False).start()
    arrived(ring_k, b_block(0, False))

    m_run[...] = jnp.full_like(m_run, FLOOR)
    m_dq[...] = jnp.full_like(m_dq, FLOOR)
    l_run[...] = jnp.zeros_like(l_run)
    dqt[...] = jnp.zeros_like(dqt)
    dqr[...] = jnp.zeros_like(dqr)

    places = lax.broadcasted_iota(jnp.int32, (RING * 4, RING * 4), 0)
    stored_at = lax.broadcasted_iota(jnp.int32, (RING * 4, RING * 4), 1)
    found = jnp.max(jnp.where(order_ref[...] == places, stored_at, 0), axis=1, keepdims=True)
    inv_v[:, 0 : RING * 4] = jnp.max(jnp.where(places == stored_at, found, 0), axis=0, keepdims=True)
    inv_copy = pltpu.make_async_copy(inv_v, inv, inv_s)
    inv_copy.start()

    def weights(keys, chunk, key_start):
        s = jnp.dot(keys, qt[...], preferred_element_type=F32) * SCALE2
        if key_start is not None:
            key_pos = key_start + lax.broadcasted_iota(jnp.int32, (CHUNK, ROWS), 0)
            lane = lax.broadcasted_iota(jnp.int32, (CHUNK, ROWS), 1)
            s = jnp.where(key_pos <= ctx * TOKENS + (lane & (TOKENS - 1)), s, FLOOR)
        m_old = m_run[...]
        m_new = jnp.maximum(m_old, jnp.max(s, axis=0, keepdims=True))
        alpha = jnp.exp2(m_old - m_new)
        p = jnp.exp2(s - m_new)
        l_run[...] = l_run[...] * alpha + jnp.sum(p, axis=0, keepdims=True)
        m_run[...] = m_new
        mst[chunk] = m_new
        pst[pl.ds(chunk * 4, 4)] = p.reshape(4, PB, ROWS)
        return p, m_new

    def level_rows(lev):
        return pl.ds(pl.multiple_of(lev * CHUNK, CHUNK), CHUNK)

    def prompt_first(lev):
        keys = pkv[level_rows(lev), 0:DIM]
        p, m_new = weights(keys, lev, None)
        alpha = jnp.exp2(m_dq[...] - m_new)
        m_dq[...] = m_new
        dp = jnp.dot(pkv[level_rows(lev), DIM:], dot[...], preferred_element_type=F32)
        g = p * (dp - delta[...])
        gst[pl.ds(lev * 4, 4)] = g.reshape(4, PB, ROWS)
        dqt[...] = dqt[...] * alpha + jnp.dot(keys.T, g.astype(BF16), preferred_element_type=F32)

    def both_sides(k, then):
        for side in range(2):
            s = 2 * k - 1 + side

            @pl.when((s >= 1) & (s < RING))
            def _():
                then(s)

    def first(k, _):
        both_sides(k, lambda s: ring_step(ring_a, s, True))
        both_sides(k, lambda s: ring_step(ring_k, s, False))

        def prompt_side(s, _):
            @pl.when((s >= 0) & (s < RING))
            def _():
                lev = level_at(s, z)
                core_arrived(lev)
                prompt_first(lev)

            return 0

        lax.fori_loop(2 * k - 1, 2 * k + 1, prompt_side, 0)
        both_sides(k - 1, lambda s: ring_step(ring_v, s, False))

        def resp_side(s, _):
            lev = level_at(s, y)

            @pl.when((s >= 0) & (s < RING) & (lev <= y))
            def _():
                weights(rkeys[level_rows(lev), :], RING + lev, lev * CHUNK)

            return 0

        lax.fori_loop(2 * k - 1, 2 * k + 1, resp_side, 0)

        return 0

    lax.fori_loop(0, HALF + 1, first, 0)
    inv_copy.wait()
    pl.semaphore_signal(token, inc=1, device_id=mirror, device_id_type=MESH)

    lane = lax.broadcasted_iota(jnp.int32, (1, ROWS), 1)
    live = ctx * TOKENS + (lane & (TOKENS - 1)) < len_ref[0]
    m_all = m_run[...]
    inv_l = jnp.where(live, 1.0 / l_run[...], 0.0)
    for i in range(2 * RING):
        factor = jnp.exp2(mst[i] - m_all) * inv_l
        for b in range(4):
            fac[4 * i + b] = factor

    def scaled(store, block):
        return (store[block] * fac[block]).astype(BF16)

    def c1_copy(lev):
        return remote(c1_send.at[lev], c1_recv.at[lev], c1_ss, c1_rs.at[lev], other_core)

    def c_term(lev, sub):
        return c1_own[lev, sub] + c1_recv[lev, sub]

    routes = ((4, 2, True, ()), (3, 1, True, ()), (3, 2, False, ()), (2, 2, True, (0, 1)),
              (2, 1, False, ()), (1, 1, True, ()), (1, 1, False, (2, 4)))

    def c_copy(m, up):
        d = 0 if up else 1
        go = routes[m][1]
        return remote(c2_send.at[d, m], c2_recv.at[d, m], c2_ss, c2_rs.at[d, m], at_z(go if up else -go))

    def c_message(m, up):
        d = 0 if up else 1
        dist, _, longer, added = routes[m]
        value = c_term(lax.rem(z + RING + (dist if up else -dist), RING), d if longer else 1 - d)
        for a in added:
            c_copy(a, up).wait_recv()
            value = value + c2_recv[d, a].astype(F32)
        c2_send[d, m] = value.astype(BF16)
        c_copy(m, up).start()

    def c_events(s):
        if s == 6:
            c1_copy(lax.rem(z + HALF, RING)).wait_recv()
            c_message(0, True)
            c_message(0, False)
        plain = {5: (3, True), 4: (3, False), 3: (2, True), 2: (2, False), 1: (1, True), 0: (1, False)}
        if s in plain:
            dist, up = plain[s]
            c1_copy(lax.rem(z + RING + (dist if up else -dist), RING)).wait_recv()
            for m in {3: (1, 2), 2: (4,), 1: (5,)}[dist]:
                c_message(m, up)

    def c_total(sub):
        d = sub
        value = c_term(z, sub)
        for m, up in ((3, d == 0), (5, d == 0), (6, d == 1)):
            value = value + c2_recv[0 if up else 1, m].astype(F32)
        return value

    holds = lax.rem(y, 2) == xl

    def rs_copy(dx, step):
        to_xh = xh if dx == 0 else 1 - xh
        to_y = lax.rem(y + step, RING)
        return remote(
            rs_send.at[to_xh, to_y], rs_recv.at[(dx * RING + step) * 2 + xl], rs_ss, rs_rs,
            (z * 4 + to_xh * 2 + core, 2 * to_y + lax.rem(to_y, 2)),
        )

    def ag_copy(step):
        return remote(ag_recv.at[y], ag_recv.at[y], ag_ss, ag_rs, at_ctx(step))

    far_first = (4, 3, 5, 2, 6, 1, 7, 0)

    def c_scatter():
        c1_copy(z).wait_recv()
        for up in (True, False):
            for m in (3, 5, 6):
                c_copy(m, up).wait_recv()
        for sub in range(2):
            value = c_total(sub).astype(BF16)
            for i in range(RING):
                r, c = i // 2, i % 2
                rs_send[sub, i] = value[r * 16 : (r + 1) * 16, c * DIM : (c + 1) * DIM]
        pl.semaphore_wait(token, 1)
        for step in far_first[:-1]:
            rs_copy(1, step).start()
            rs_copy(0, step).start()
        rs_copy(1, 0).start()

        @pl.when(holds)
        def _():
            rs_recv[xl] = rs_send[xh, y]

        @pl.when(jnp.logical_not(holds))
        def _():
            rs_copy(0, 0).start()

    def c_gather():
        @pl.when(holds)
        def _():
            rest = rs_recv.at[0 : 4 * RING - 1]
            remote(rest, rest, rs_ss, rs_rs, other_core).wait_recv()
            piece = rs_recv[0].astype(F32)
            for i in range(1, 4 * RING):
                piece = piece + rs_recv[i].astype(F32)
            ag_recv[y] = piece.astype(BF16)
            for step in (8, 7, 9, 6, 10, 5, 11, 4, 12, 3, 13, 2, 14, 1, 15):
                ag_copy(step).start()

    def c_finish():
        @pl.when(holds)
        def _():
            rest = ag_recv.at[0 : RING - 1]
            remote(rest, rest, ag_ss, ag_rs, other_core).wait_recv()

        @pl.when(jnp.logical_not(holds))
        def _():
            remote(ag_recv, ag_recv, ag_ss, ag_rs, other_core).wait_recv()

        for c, out in ((0, pdk_ref), (1, pdv_ref)):
            for r in range(RING // 2):
                out[r * 16 : (r + 1) * 16, :] = ag_recv[2 * r + c]

    def d_copy(j, kv, up):
        d = 0 if up else 1
        at = at_y(1 if up else -1)
        if j == 1:
            return remote(d_send.at[d, 0, kv, d], d_recv.at[d, 0, kv, d], d_ss.at[0], d_rs.at[d, 0, kv], at)
        return remote(d_send.at[d, j - 1, kv], d_recv.at[d, j - 1, kv], d_ss.at[1], d_rs.at[d, j - 1, kv], at)

    def d_step(j):
        dist = HALF + 1 - j
        for kv in range(2):
            for up in (True, False):
                d = 0 if up else 1
                if j > 1:
                    d_copy(j - 1, kv, up).wait_recv()
                lev = lax.rem(y + RING + (dist if up else -dist), RING)
                for sub in range(2):
                    begins = sub == d
                    if j == 1 and not begins:
                        continue
                    value = d_own[lev, kv, sub]
                    if j > 2 or (j == 2 and begins):
                        value = value + d_recv[d, j - 2, kv, sub].astype(F32)
                    d_send[d, j - 1, kv, sub] = value.astype(BF16)
                d_copy(j, kv, up).start()

    def prompt_second(i, _):
        s = RING - 1 - i
        lev = level_at(s, z)
        ps, gs = [], []
        for b in range(4):
            stored = inv[0, lev * 4 + b]
            ps.append(scaled(pst, stored))
            gs.append(scaled(gst, stored))
        dv = jnp.dot(jnp.concatenate(ps, axis=0), dos[...], preferred_element_type=F32)
        dk = jnp.dot(jnp.concatenate(gs, axis=0), qs[...], preferred_element_type=F32) * SCALE
        for sub in range(2):
            for c in range(2):
                rows = slice((sub * 2 + c) * PB, (sub * 2 + c + 1) * PB)

                @pl.when(core == c)
                def _():
                    c1_own[lev, sub, :, 0:DIM] = dk[rows]
                    c1_own[lev, sub, :, DIM:] = dv[rows]

                @pl.when(core != c)
                def _():
                    c1_send[lev, sub, :, 0:DIM] = dk[rows]
                    c1_send[lev, sub, :, DIM:] = dv[rows]

        c1_copy(lev).start()

        for when in range(RING - 1):

            @pl.when(s == when)
            def _():
                c_events(when)

        return 0

    lax.fori_loop(0, RING, prompt_second, 0)
    arrived(ring_v, b_block(0, False))
    ring_step(ring_v, jnp.int32(RING - 1), False)

    def resp_second(i, _):
        s = RING - 1 - i
        lev = level_at(s, y)

        @pl.when(lev <= y)
        def _():
            keys = rkeys[level_rows(lev), :]
            dp = jnp.dot(rvalues[level_rows(lev), :], dot[...], preferred_element_type=F32)
            block = (RING + lev) * 4
            p = pst[pl.ds(block, 4)].reshape(CHUNK, ROWS) * fac[block]
            g = (p * (dp - delta[...])).astype(BF16)
            dv = jnp.dot(p.astype(BF16), dos[...], preferred_element_type=F32)
            dk = jnp.dot(g, qs[...], preferred_element_type=F32) * SCALE
            dqr[...] += jnp.dot(keys.T, g, preferred_element_type=F32)
            for sub in range(2):
                rows = slice(sub * RB, (sub + 1) * RB)
                d_own[lev, 0, sub] = dk[rows]
                d_own[lev, 1, sub] = dv[rows]

        @pl.when(lev > y)
        def _():
            d_own[lev] = jnp.zeros((2, 2, RB, DIM), F32)

        @pl.when(s == 7)
        def _():
            d_step(1)
            c_message(3, True)
            c_message(3, False)

        @pl.when(s == 6)
        def _():
            c_message(6, True)
            c_message(6, False)

        @pl.when(s == 3)
        def _():
            c_scatter()
            d_step(2)

        return 0

    lax.fori_loop(0, RING, resp_second, 0)

    dq_factor = jnp.exp2(m_dq[...] - m_all) * inv_l
    for h in range(HEADS):
        lanes = slice(h * DIM, (h + 1) * DIM)
        dq = dqt[:, lanes] * dq_factor[:, lanes] + dqr[:, lanes]
        dq_ref[:, lanes] = (dq * SCALE).T.astype(BF16)

    d_step(3)

    c_gather()
    d_step(4)

    for kv in range(2):
        for up in (True, False):
            d_copy(HALF, kv, up).wait_recv()
        for sub in range(2):
            d_tot[kv, sub] = d_own[y, kv, sub] + sum(d_recv[d, HALF - 1, kv, sub].astype(F32) for d in range(2))
        d_xsend[kv] = d_tot[kv, 1 - xl].astype(BF16)

    def dx_copy(kv):
        return remote(d_xsend.at[kv], d_xrecv.at[kv], dx_ss, dx_rs.at[kv], x_pair)

    for kv in range(2):
        dx_copy(kv).start()
    for kv, out in ((0, rdk_ref), (1, rdv_ref)):
        dx_copy(kv).wait_recv()
        out[...] = (d_tot[kv, xl] + d_xrecv[kv].astype(F32)).astype(BF16)

    c_finish()

    all_sent(pkv.at[0 : 31 * PB], a_ss)
    all_sent(rkeys.at[0 : 15 * RB], bk_ss)
    all_sent(rvalues.at[0 : 15 * RB], bv_ss)
    all_sent(c1_send, c1_ss)
    all_sent(c2_send, c2_ss)
    all_sent(d_send.at[0, 0], d_ss.at[0])
    all_sent(d_send.at[:, 1:HALF], d_ss.at[1])
    all_sent(d_xsend, dx_ss)

    @pl.when(holds)
    def _():
        all_sent(rs_recv.at[0:15], rs_ss)
        all_sent(rs_recv.at[0:15], ag_ss)

    @pl.when(jnp.logical_not(holds))
    def _():
        all_sent(rs_recv.at[0:16], rs_ss)


def hand_over(*refs):
    n = len(refs) // 2
    for i in range(n):
        refs[n + i][...] = refs[i][...]


def local(query, resp_key, resp_value, prompt_key, prompt_value, saved_out, out_grad, resp_len, prompt_order):
    vmem = pl.BlockSpec(memory_space=pltpu.VMEM)
    smem = pl.BlockSpec(memory_space=pltpu.SMEM)
    dma = pltpu.SemaphoreType.DMA
    wide = 2 * DIM
    outs = pl.pallas_call(
        body,
        out_shape=(
            jax.ShapeDtypeStruct((TOKENS, HEADS * DIM), BF16),
            jax.ShapeDtypeStruct((RB, DIM), BF16),
            jax.ShapeDtypeStruct((RB, DIM), BF16),
            jax.ShapeDtypeStruct((PB, DIM), BF16),
            jax.ShapeDtypeStruct((PB, DIM), BF16),
        ),
        in_specs=[pl.BlockSpec(memory_space=pl.ANY)] * 7 + [smem, vmem],
        out_specs=(vmem,) * 5,
        scratch_shapes=[
            pltpu.VMEM((TOKENS, ROWS), BF16),
            pltpu.VMEM((TOKENS, ROWS), BF16),
            pltpu.VMEM((TOKENS, ROWS), BF16),
            pltpu.VMEM((RING * CHUNK, wide), BF16),
            pltpu.VMEM((RING * CHUNK, DIM), BF16),
            pltpu.VMEM((RING * CHUNK, DIM), BF16),
            pltpu.VMEM((ROWS, DIM), BF16),
            pltpu.VMEM((ROWS, DIM), BF16),
            pltpu.VMEM((DIM, ROWS), BF16),
            pltpu.VMEM((DIM, ROWS), BF16),
            pltpu.VMEM((1, ROWS), F32),
            pltpu.VMEM((2 * RING * 4, PB, ROWS), F32),
            pltpu.VMEM((RING * 4, PB, ROWS), F32),
            pltpu.VMEM((2 * RING, 1, ROWS), F32),
            pltpu.VMEM((1, ROWS), F32),
            pltpu.VMEM((1, ROWS), F32),
            pltpu.VMEM((1, ROWS), F32),
            pltpu.VMEM((2 * RING * 4, 1, ROWS), F32),
            pltpu.VMEM((DIM, ROWS), F32),
            pltpu.VMEM((DIM, ROWS), F32),
            pltpu.VMEM((1, DIM), jnp.int32),
            pltpu.SMEM((1, DIM), jnp.int32),
            pltpu.VMEM((RING, 2, PB, wide), F32),
            pltpu.VMEM((RING, 2, PB, wide), F32),
            pltpu.VMEM((RING, 2, PB, wide), F32),
            pltpu.VMEM((2, 7, PB, wide), BF16),
            pltpu.VMEM((2, 7, PB, wide), BF16),
            pltpu.VMEM((2, RING, 16, DIM), BF16),
            pltpu.VMEM((4 * RING, 16, DIM), BF16),
            pltpu.VMEM((RING, 16, DIM), BF16),
            pltpu.VMEM((RING, 2, 2, RB, DIM), F32),
            pltpu.VMEM((2, HALF, 2, 2, RB, DIM), BF16),
            pltpu.VMEM((2, HALF, 2, 2, RB, DIM), BF16),
            pltpu.VMEM((2, 2, RB, DIM), F32),
            pltpu.VMEM((2, RB, DIM), BF16),
            pltpu.VMEM((2, RB, DIM), BF16),
            dma((7,)),
            dma,
            dma((RING * 2,)),
            dma((RING,)),
            dma,
            dma((GROUP,)),
            dma,
            dma((GROUP,)),
            dma,
            dma,
            dma((RING,)),
            dma,
            dma((2, 7)),
            dma,
            dma,
            dma,
            dma,
            dma((2,)),
            dma((2, HALF, 2)),
            dma,
            dma((2,)),
            pltpu.SemaphoreType.REGULAR,
        ],
        compiler_params=pltpu.CompilerParams(
            collective_id=0, has_side_effects=True, vmem_limit_bytes=VMEM
        ),
        name="attention_backward",
    )(
        query[0], resp_key[0], resp_value[0], prompt_key, prompt_value,
        saved_out[0], out_grad[0], resp_len, prompt_order[None],
    )
    outs = pl.pallas_call(
        hand_over,
        out_shape=tuple(jax.ShapeDtypeStruct(out.shape, out.dtype) for out in outs),
        in_specs=[vmem] * 5,
        out_specs=(vmem,) * 5,
        compiler_params=pltpu.CompilerParams(vmem_limit_bytes=VMEM),
        name="hand_over",
    )(*outs)
    return (outs[0][None], outs[1][None], outs[2][None], outs[3], outs[4])


def solution(mesh):
    token = P("resp", "ctx", None)
    block = P("resp", None)
    return jax.shard_map(
        local,
        mesh=mesh,
        in_specs=(token, token, token, block, block, token, token, P("resp"), P()),
        out_specs=(token, token, token, block, block),
        check_vma=False,
    )
```

```python
import math

import jax
import jax.numpy as jnp
from jax import lax
from jax.experimental import pallas as pl
from jax.experimental.pallas import tpu as pltpu
from jax.sharding import PartitionSpec as P

MESH = pl.DeviceIdType.MESH
HEADS = 8
DIM = 128
SCALE = DIM ** (-0.5)
SCALE2 = SCALE * math.log2(math.e)
FLOOR = -1e30
RING = 8
HALF = RING // 2
GROUP = 16
PB = 64
RB = 128
CHUNK = 256
TOKENS = 128
ROWS = TOKENS * HEADS
VMEM = 56 * 1024 * 1024
F32 = jnp.float32
BF16 = jnp.bfloat16


def level_at(s, idx):
    k = (s + 1) // 2
    odd = lax.rem(s, 2)
    return lax.rem(idx + RING + k - 2 * k * odd, RING)


def body(
    q_hbm, rk_hbm, rv_hbm, pk_hbm, pv_hbm, o_hbm, do_hbm, len_ref, order_ref,
    dq_ref, rdk_ref, rdv_ref, pdk_ref, pdv_ref,
    q_ref, o_ref, do_ref, pkv, rkeys, rvalues, qs, dos, qt, dot, delta, pst, gst, mst, m_run, m_dq, l_run, fac, dqt, dqr, inv_v, inv,
    c1_own, c1_send, c1_recv, c2_send, c2_recv,
    rs_send, rs_recv, ag_recv,
    d_own, d_send, d_recv, d_tot, d_xsend, d_xrecv,
    in_s, inv_s, a_rs, a_cr, a_ss, bk_rs, bk_ss, bv_rs, bv_ss,
    c1_ss, c1_rs, c2_ss, c2_rs, rs_ss, rs_rs, ag_ss, ag_rs,
    d_ss, d_rs, dx_ss, dx_rs, token,
):
    resp = lax.axis_index("resp")
    ctx = lax.axis_index("ctx")
    z, xh, core = resp // 4, lax.rem(resp // 2, 2), lax.rem(resp, 2)
    y, xl = ctx // 2, lax.rem(ctx, 2)
    z_low = resp - z * 4

    def at_z(step, across=False):
        low, c = (z_low + 2 - 4 * xh, ctx + 1 - 2 * xl) if across else (z_low, ctx)
        return (lax.rem(z + RING + step, RING) * 4 + low, c)

    def at_y(step, across=False):
        return (resp, lax.rem(y + RING + step, RING) * 2 + (1 - xl if across else xl))

    other_core = (resp + 1 - 2 * core, ctx)
    mirror = (resp + 2 - 4 * xh, ctx + 1 - 2 * xl)
    x_pair = (resp, ctx + 1 - 2 * xl)

    def at_ctx(step):
        return (resp, lax.rem(ctx + step, GROUP))

    def remote(src, dst, ss, rs, device):
        return pltpu.make_async_remote_copy(
            src_ref=src, dst_ref=dst, send_sem=ss, recv_sem=rs,
            device_id=device, device_id_type=MESH,
        )

    barrier = pltpu.get_barrier_semaphore()
    partners = [other_core, mirror, x_pair]
    partners += [at(step, across) for at in (at_z, at_y) for step in (1, -1) for across in (False, True)]
    for device in partners:
        pl.semaphore_signal(barrier, inc=1, device_id=device, device_id_type=MESH)

    p_rows = pl.ds(pl.multiple_of(resp * PB, PB), PB)
    r_rows = pl.ds(pl.multiple_of(ctx * RB, RB), RB)
    moves = (
        (pk_hbm, pkv.at[p_rows, 0:DIM]), (pv_hbm, pkv.at[p_rows, DIM : 2 * DIM]),
        (rk_hbm, rkeys.at[r_rows]), (rv_hbm, rvalues.at[r_rows]),
        (q_hbm, q_ref), (do_hbm, do_ref), (o_hbm, o_ref),
    )
    reads = [pltpu.make_async_copy(src, dst, in_s.at[i]) for i, (src, dst) in enumerate(moves)]
    for read in reads:
        read.start()
    for read in reads[:4]:
        read.wait()
    pl.semaphore_wait(barrier, len(partners))

    def p_block(lev, sub, c):
        return lev * 4 + sub * 2 + c

    def p_slot(b):
        return pkv.at[pl.ds(pl.multiple_of(b * PB, PB), PB)]

    def r_slot(buffer):
        return lambda b: buffer.at[pl.ds(pl.multiple_of(b * RB, RB), RB)]

    def a_block(s, own):
        return p_block(level_at(s, z), xh if own else 1 - xh, core)

    def b_block(s, own):
        return level_at(s, y) * 2 + (xl if own else 1 - xl)

    ring_a = (p_slot, a_block, lambda b: a_rs.at[b // 2], a_ss, at_z)
    ring_k = (r_slot(rkeys), b_block, lambda b: bk_rs.at[b], bk_ss, at_y)
    ring_v = (r_slot(rvalues), b_block, lambda b: bv_rs.at[b], bv_ss, at_y)

    def ring_copy(ring, s, own, device):
        slot, block, rs, ss, _ = ring
        b = block(s, own)
        return remote(slot(b), slot(b), ss, rs(b), device)

    def arrived(ring, b):
        slot, _, rs, ss, _ = ring
        remote(slot(b), slot(b), ss, rs(b), other_core).wait_recv()

    def core_copy(s, own):
        b = a_block(s, own)
        return remote(p_slot(b), p_slot(b), a_ss, a_cr.at[b // 4], other_core)

    def core_arrived(lev):
        both = pkv.at[pl.ds(pl.multiple_of(lev * CHUNK, CHUNK), 2 * PB)]
        remote(both, both, a_ss, a_cr.at[lev], other_core).wait_recv()

    def all_sent(ref, ss):
        remote(ref, ref, ss, dx_rs.at[0], other_core).wait_send()

    def hops(ring, s, own):
        k = (s + 1) // 2
        odd = lax.rem(s, 2) == 1
        up_limit, down_limit = (HALF, HALF - 1) if own else (HALF - 1, HALF)

        @pl.when(odd & (k < up_limit))
        def _():
            ring_copy(ring, s, own, ring[4](1)).start()

        @pl.when(jnp.logical_not(odd) & (k < down_limit))
        def _():
            ring_copy(ring, s, own, ring[4](-1)).start()

    def ring_step(ring, s, own):
        arrived(ring, ring[1](s, own))
        hops(ring, s, own)
        if ring is ring_a:
            core_copy(s, own).start()

    for across in (False, True):
        for ring in (ring_a, ring_k):
            for step in (1, -1):
                ring_copy(ring, 0, True, ring[4](step, across)).start()
    core_copy(0, True).start()
    ring_copy(ring_a, 0, True, mirror).start()
    ring_copy(ring_k, 0, True, x_pair).start()
    for across in (False, True):
        for step in (1, -1):
            ring_copy(ring_v, 0, True, at_y(step, across)).start()
    ring_copy(ring_v, 0, True, x_pair).start()

    def prepare(h):
        lanes = slice(h * DIM, (h + 1) * DIM)
        q = q_ref[:, lanes]
        do = do_ref[:, lanes]
        qs[lanes, :] = q
        dos[lanes, :] = do
        qt[:, lanes] = q.T
        dot[:, lanes] = do.T
        product = do.astype(F32) * o_ref[:, lanes].astype(F32)
        delta[:, lanes] = jnp.sum(product.T, axis=0, keepdims=True)

    for read in reads[4:]:
        read.wait()
    for h in range(HEADS):
        prepare(h)
    arrived(ring_a, a_block(0, False))
    core_copy(0, False).start()
    arrived(ring_k, b_block(0, False))

    m_run[...] = jnp.full_like(m_run, FLOOR)
    m_dq[...] = jnp.full_like(m_dq, FLOOR)
    l_run[...] = jnp.zeros_like(l_run)
    dqt[...] = jnp.zeros_like(dqt)
    dqr[...] = jnp.zeros_like(dqr)

    places = lax.broadcasted_iota(jnp.int32, (RING * 4, RING * 4), 0)
    stored_at = lax.broadcasted_iota(jnp.int32, (RING * 4, RING * 4), 1)
    found = jnp.max(jnp.where(order_ref[...] == places, stored_at, 0), axis=1, keepdims=True)
    inv_v[:, 0 : RING * 4] = jnp.max(jnp.where(places == stored_at, found, 0), axis=0, keepdims=True)
    inv_copy = pltpu.make_async_copy(inv_v, inv, inv_s)
    inv_copy.start()

    def weights(keys, chunk, key_start):
        s = jnp.dot(keys, qt[...], preferred_element_type=F32) * SCALE2
        if key_start is not None:
            key_pos = key_start + lax.broadcasted_iota(jnp.int32, (CHUNK, ROWS), 0)
            lane = lax.broadcasted_iota(jnp.int32, (CHUNK, ROWS), 1)
            s = jnp.where(key_pos <= ctx * TOKENS + (lane & (TOKENS - 1)), s, FLOOR)
        m_old = m_run[...]
        m_new = jnp.maximum(m_old, jnp.max(s, axis=0, keepdims=True))
        alpha = jnp.exp2(m_old - m_new)
        p = jnp.exp2(s - m_new)
        l_run[...] = l_run[...] * alpha + jnp.sum(p, axis=0, keepdims=True)
        m_run[...] = m_new
        mst[chunk] = m_new
        pst[pl.ds(chunk * 4, 4)] = p.reshape(4, PB, ROWS)
        return p, m_new

    def level_rows(lev):
        return pl.ds(pl.multiple_of(lev * CHUNK, CHUNK), CHUNK)

    def prompt_first(lev):
        keys = pkv[level_rows(lev), 0:DIM]
        p, m_new = weights(keys, lev, None)
        alpha = jnp.exp2(m_dq[...] - m_new)
        m_dq[...] = m_new
        dp = jnp.dot(pkv[level_rows(lev), DIM:], dot[...], preferred_element_type=F32)
        g = p * (dp - delta[...])
        gst[pl.ds(lev * 4, 4)] = g.reshape(4, PB, ROWS)
        dqt[...] = dqt[...] * alpha + jnp.dot(keys.T, g.astype(BF16), preferred_element_type=F32)

    def both_sides(k, then):
        for side in range(2):
            s = 2 * k - 1 + side

            @pl.when((s >= 1) & (s < RING))
            def _():
                then(s)

    def first(k, _):
        for own in (True, False):
            for ring in (ring_a, ring_k):
                both_sides(k + 1, lambda s: ring_step(ring, s, own))

        def prompt_side(s, _):
            @pl.when((s >= 0) & (s < RING))
            def _():
                lev = level_at(s, z)
                core_arrived(lev)
                prompt_first(lev)

            return 0

        lax.fori_loop(2 * k - 1, 2 * k + 1, prompt_side, 0)
        for own in (True, False):
            both_sides(k + 1, lambda s: ring_step(ring_v, s, own))

        def resp_side(s, _):
            lev = level_at(s, y)

            @pl.when((s >= 0) & (s < RING) & (lev <= y))
            def _():
                weights(rkeys[level_rows(lev), :], RING + lev, lev * CHUNK)

            return 0

        lax.fori_loop(2 * k - 1, 2 * k + 1, resp_side, 0)

        return 0

    lax.fori_loop(0, HALF + 1, first, 0)
    arrived(ring_v, b_block(0, False))
    inv_copy.wait()
    pl.semaphore_signal(token, inc=1, device_id=mirror, device_id_type=MESH)

    lane = lax.broadcasted_iota(jnp.int32, (1, ROWS), 1)
    live = ctx * TOKENS + (lane & (TOKENS - 1)) < len_ref[0]
    m_all = m_run[...]
    inv_l = jnp.where(live, 1.0 / l_run[...], 0.0)
    for i in range(2 * RING):
        factor = jnp.exp2(mst[i] - m_all) * inv_l
        for b in range(4):
            fac[4 * i + b] = factor

    def scaled(store, block):
        return (store[block] * fac[block]).astype(BF16)

    def c1_copy(lev):
        return remote(c1_send.at[lev], c1_recv.at[lev], c1_ss, c1_rs.at[lev], other_core)

    def c_term(lev, sub):
        return c1_own[lev, sub] + c1_recv[lev, sub]

    routes = ((4, 2, True, ()), (3, 1, True, ()), (3, 2, False, ()), (2, 2, True, (0, 1)),
              (2, 1, False, ()), (1, 1, True, ()), (1, 1, False, (2, 4)))

    def c_copy(m, up):
        d = 0 if up else 1
        go = routes[m][1]
        return remote(c2_send.at[d, m], c2_recv.at[d, m], c2_ss, c2_rs.at[d, m], at_z(go if up else -go))

    def c_message(m, up):
        d = 0 if up else 1
        dist, _, longer, added = routes[m]
        value = c_term(lax.rem(z + RING + (dist if up else -dist), RING), d if longer else 1 - d)
        for a in added:
            c_copy(a, up).wait_recv()
            value = value + c2_recv[d, a].astype(F32)
        c2_send[d, m] = value.astype(BF16)
        c_copy(m, up).start()

    def c_events(s):
        if s == 6:
            c1_copy(lax.rem(z + HALF, RING)).wait_recv()
            c_message(0, True)
            c_message(0, False)
        plain = {5: (3, True), 4: (3, False), 3: (2, True), 2: (2, False), 1: (1, True), 0: (1, False)}
        if s in plain:
            dist, up = plain[s]
            c1_copy(lax.rem(z + RING + (dist if up else -dist), RING)).wait_recv()
            for m in {3: (1, 2), 2: (4,), 1: (5,)}[dist]:
                c_message(m, up)

    def c_total(sub):
        d = sub
        value = c_term(z, sub)
        for m, up in ((3, d == 0), (5, d == 0), (6, d == 1)):
            value = value + c2_recv[0 if up else 1, m].astype(F32)
        return value

    holds = lax.rem(y, 2) == xl

    def rs_copy(dx, step):
        to_xh = xh if dx == 0 else 1 - xh
        to_y = lax.rem(y + step, RING)
        return remote(
            rs_send.at[to_xh, to_y], rs_recv.at[(dx * RING + step) * 2 + xl], rs_ss, rs_rs,
            (z * 4 + to_xh * 2 + core, 2 * to_y + lax.rem(to_y, 2)),
        )

    def ag_copy(step):
        return remote(ag_recv.at[y], ag_recv.at[y], ag_ss, ag_rs, at_ctx(step))

    far_first = (4, 3, 5, 2, 6, 1, 7, 0)

    def c_scatter():
        c1_copy(z).wait_recv()
        for up in (True, False):
            for m in (3, 5, 6):
                c_copy(m, up).wait_recv()
        for sub in range(2):
            value = c_total(sub).astype(BF16)
            for i in range(RING):
                r, c = i // 2, i % 2
                rs_send[sub, i] = value[r * 16 : (r + 1) * 16, c * DIM : (c + 1) * DIM]
        pl.semaphore_wait(token, 1)
        for step in far_first[:-1]:
            rs_copy(1, step).start()
            rs_copy(0, step).start()
        rs_copy(1, 0).start()

        @pl.when(holds)
        def _():
            rs_recv[xl] = rs_send[xh, y]

        @pl.when(jnp.logical_not(holds))
        def _():
            rs_copy(0, 0).start()

    def c_gather():
        @pl.when(holds)
        def _():
            rest = rs_recv.at[0 : 4 * RING - 1]
            remote(rest, rest, rs_ss, rs_rs, other_core).wait_recv()
            piece = rs_recv[0].astype(F32)
            for i in range(1, 4 * RING):
                piece = piece + rs_recv[i].astype(F32)
            ag_recv[y] = piece.astype(BF16)
            for step in (8, 7, 9, 6, 10, 5, 11, 4, 12, 3, 13, 2, 14, 1, 15):
                ag_copy(step).start()

    def c_finish():
        @pl.when(holds)
        def _():
            rest = ag_recv.at[0 : RING - 1]
            remote(rest, rest, ag_ss, ag_rs, other_core).wait_recv()

        @pl.when(jnp.logical_not(holds))
        def _():
            remote(ag_recv, ag_recv, ag_ss, ag_rs, other_core).wait_recv()

        for c, out in ((0, pdk_ref), (1, pdv_ref)):
            for r in range(RING // 2):
                out[r * 16 : (r + 1) * 16, :] = ag_recv[2 * r + c]

    def d_copy(j, kv, up):
        d = 0 if up else 1
        at = at_y(1 if up else -1)
        if j == 1:
            return remote(d_send.at[d, 0, kv, d], d_recv.at[d, 0, kv, d], d_ss.at[0], d_rs.at[d, 0, kv], at)
        return remote(d_send.at[d, j - 1, kv], d_recv.at[d, j - 1, kv], d_ss.at[1], d_rs.at[d, j - 1, kv], at)

    def d_step(j):
        dist = HALF + 1 - j
        for kv in range(2):
            for up in (True, False):
                d = 0 if up else 1
                if j > 1:
                    d_copy(j - 1, kv, up).wait_recv()
                lev = lax.rem(y + RING + (dist if up else -dist), RING)
                for sub in range(2):
                    begins = sub == d
                    if j == 1 and not begins:
                        continue
                    value = d_own[lev, kv, sub]
                    if j > 2 or (j == 2 and begins):
                        value = value + d_recv[d, j - 2, kv, sub].astype(F32)
                    d_send[d, j - 1, kv, sub] = value.astype(BF16)
                d_copy(j, kv, up).start()

    def resp_level(s):
        lev = level_at(s, y)

        @pl.when(lev <= y)
        def _():
            keys = rkeys[level_rows(lev), :]
            dp = jnp.dot(rvalues[level_rows(lev), :], dot[...], preferred_element_type=F32)
            block = (RING + lev) * 4
            p = pst[pl.ds(block, 4)].reshape(CHUNK, ROWS) * fac[block]
            g = (p * (dp - delta[...])).astype(BF16)
            dv = jnp.dot(p.astype(BF16), dos[...], preferred_element_type=F32)
            dk = jnp.dot(g, qs[...], preferred_element_type=F32) * SCALE
            dqr[...] += jnp.dot(keys.T, g, preferred_element_type=F32)
            for sub in range(2):
                rows = slice(sub * RB, (sub + 1) * RB)
                d_own[lev, 0, sub] = dk[rows]
                d_own[lev, 1, sub] = dv[rows]

        @pl.when(lev > y)
        def _():
            d_own[lev] = jnp.zeros((2, 2, RB, DIM), F32)

    def prompt_second(i, _):
        s = RING - 1 - i
        lev = level_at(s, z)
        ps, gs = [], []
        for b in range(4):
            stored = inv[0, lev * 4 + b]
            ps.append(scaled(pst, stored))
            gs.append(scaled(gst, stored))
        dv = jnp.dot(jnp.concatenate(ps, axis=0), dos[...], preferred_element_type=F32)
        dk = jnp.dot(jnp.concatenate(gs, axis=0), qs[...], preferred_element_type=F32) * SCALE
        for sub in range(2):
            for c in range(2):
                rows = slice((sub * 2 + c) * PB, (sub * 2 + c + 1) * PB)

                @pl.when(core == c)
                def _():
                    c1_own[lev, sub, :, 0:DIM] = dk[rows]
                    c1_own[lev, sub, :, DIM:] = dv[rows]

                @pl.when(core != c)
                def _():
                    c1_send[lev, sub, :, 0:DIM] = dk[rows]
                    c1_send[lev, sub, :, DIM:] = dv[rows]

        c1_copy(lev).start()

        for when in range(RING - 1):

            @pl.when(s == when)
            def _():
                c_events(when)

        @pl.when(s == 5)
        def _():
            resp_level(RING - 1)
            d_step(1)

        return 0

    lax.fori_loop(0, RING, prompt_second, 0)
    c_message(3, True)
    c_message(3, False)

    def resp_second(i, _):
        s = RING - 2 - i
        resp_level(s)

        @pl.when(s == 6)
        def _():
            c_message(6, True)
            c_message(6, False)

        @pl.when(s == 5)
        def _():
            d_step(2)

        @pl.when(s == 3)
        def _():
            c_scatter()

        return 0

    lax.fori_loop(0, RING - 1, resp_second, 0)

    dq_factor = jnp.exp2(m_dq[...] - m_all) * inv_l
    for h in range(HEADS):
        lanes = slice(h * DIM, (h + 1) * DIM)
        dq = dqt[:, lanes] * dq_factor[:, lanes] + dqr[:, lanes]
        dq_ref[:, lanes] = (dq * SCALE).T.astype(BF16)

    d_step(3)

    d_step(4)
    c_gather()

    for kv in range(2):
        for up in (True, False):
            d_copy(HALF, kv, up).wait_recv()
        for sub in range(2):
            d_tot[kv, sub] = d_own[y, kv, sub] + sum(d_recv[d, HALF - 1, kv, sub].astype(F32) for d in range(2))
        d_xsend[kv] = d_tot[kv, 1 - xl].astype(BF16)

    def dx_copy(kv):
        return remote(d_xsend.at[kv], d_xrecv.at[kv], dx_ss, dx_rs.at[kv], x_pair)

    for kv in range(2):
        dx_copy(kv).start()
    for kv, out in ((0, rdk_ref), (1, rdv_ref)):
        dx_copy(kv).wait_recv()
        out[...] = (d_tot[kv, xl] + d_xrecv[kv].astype(F32)).astype(BF16)

    c_finish()

    all_sent(pkv.at[0 : 31 * PB], a_ss)
    all_sent(rkeys.at[0 : 15 * RB], bk_ss)
    all_sent(rvalues.at[0 : 15 * RB], bv_ss)
    all_sent(c1_send, c1_ss)
    all_sent(c2_send, c2_ss)
    all_sent(d_send.at[0, 0], d_ss.at[0])
    all_sent(d_send.at[:, 1:HALF], d_ss.at[1])
    all_sent(d_xsend, dx_ss)

    @pl.when(holds)
    def _():
        all_sent(rs_recv.at[0:15], rs_ss)
        all_sent(rs_recv.at[0:15], ag_ss)

    @pl.when(jnp.logical_not(holds))
    def _():
        all_sent(rs_recv.at[0:16], rs_ss)


def hand_over(*refs):
    n = len(refs) // 2
    for i in range(n):
        refs[n + i][...] = refs[i][...]


def local(query, resp_key, resp_value, prompt_key, prompt_value, saved_out, out_grad, resp_len, prompt_order):
    vmem = pl.BlockSpec(memory_space=pltpu.VMEM)
    smem = pl.BlockSpec(memory_space=pltpu.SMEM)
    dma = pltpu.SemaphoreType.DMA
    wide = 2 * DIM
    outs = pl.pallas_call(
        body,
        out_shape=(
            jax.ShapeDtypeStruct((TOKENS, HEADS * DIM), BF16),
            jax.ShapeDtypeStruct((RB, DIM), BF16),
            jax.ShapeDtypeStruct((RB, DIM), BF16),
            jax.ShapeDtypeStruct((PB, DIM), BF16),
            jax.ShapeDtypeStruct((PB, DIM), BF16),
        ),
        in_specs=[pl.BlockSpec(memory_space=pl.ANY)] * 7 + [smem, vmem],
        out_specs=(vmem,) * 5,
        scratch_shapes=[
            pltpu.VMEM((TOKENS, ROWS), BF16),
            pltpu.VMEM((TOKENS, ROWS), BF16),
            pltpu.VMEM((TOKENS, ROWS), BF16),
            pltpu.VMEM((RING * CHUNK, wide), BF16),
            pltpu.VMEM((RING * CHUNK, DIM), BF16),
            pltpu.VMEM((RING * CHUNK, DIM), BF16),
            pltpu.VMEM((ROWS, DIM), BF16),
            pltpu.VMEM((ROWS, DIM), BF16),
            pltpu.VMEM((DIM, ROWS), BF16),
            pltpu.VMEM((DIM, ROWS), BF16),
            pltpu.VMEM((1, ROWS), F32),
            pltpu.VMEM((2 * RING * 4, PB, ROWS), F32),
            pltpu.VMEM((RING * 4, PB, ROWS), F32),
            pltpu.VMEM((2 * RING, 1, ROWS), F32),
            pltpu.VMEM((1, ROWS), F32),
            pltpu.VMEM((1, ROWS), F32),
            pltpu.VMEM((1, ROWS), F32),
            pltpu.VMEM((2 * RING * 4, 1, ROWS), F32),
            pltpu.VMEM((DIM, ROWS), F32),
            pltpu.VMEM((DIM, ROWS), F32),
            pltpu.VMEM((1, DIM), jnp.int32),
            pltpu.SMEM((1, DIM), jnp.int32),
            pltpu.VMEM((RING, 2, PB, wide), F32),
            pltpu.VMEM((RING, 2, PB, wide), F32),
            pltpu.VMEM((RING, 2, PB, wide), F32),
            pltpu.VMEM((2, 7, PB, wide), BF16),
            pltpu.VMEM((2, 7, PB, wide), BF16),
            pltpu.VMEM((2, RING, 16, DIM), BF16),
            pltpu.VMEM((4 * RING, 16, DIM), BF16),
            pltpu.VMEM((RING, 16, DIM), BF16),
            pltpu.VMEM((RING, 2, 2, RB, DIM), F32),
            pltpu.VMEM((2, HALF, 2, 2, RB, DIM), BF16),
            pltpu.VMEM((2, HALF, 2, 2, RB, DIM), BF16),
            pltpu.VMEM((2, 2, RB, DIM), F32),
            pltpu.VMEM((2, RB, DIM), BF16),
            pltpu.VMEM((2, RB, DIM), BF16),
            dma((7,)),
            dma,
            dma((RING * 2,)),
            dma((RING,)),
            dma,
            dma((GROUP,)),
            dma,
            dma((GROUP,)),
            dma,
            dma,
            dma((RING,)),
            dma,
            dma((2, 7)),
            dma,
            dma,
            dma,
            dma,
            dma((2,)),
            dma((2, HALF, 2)),
            dma,
            dma((2,)),
            pltpu.SemaphoreType.REGULAR,
        ],
        compiler_params=pltpu.CompilerParams(
            collective_id=0, has_side_effects=True, vmem_limit_bytes=VMEM
        ),
        name="attention_backward",
    )(
        query[0], resp_key[0], resp_value[0], prompt_key, prompt_value,
        saved_out[0], out_grad[0], resp_len, prompt_order[None],
    )
    outs = pl.pallas_call(
        hand_over,
        out_shape=tuple(jax.ShapeDtypeStruct(out.shape, out.dtype) for out in outs),
        in_specs=[vmem] * 5,
        out_specs=(vmem,) * 5,
        compiler_params=pltpu.CompilerParams(vmem_limit_bytes=VMEM),
        name="hand_over",
    )(*outs)
    return (outs[0][None], outs[1][None], outs[2][None], outs[3], outs[4])


def solution(mesh):
    token = P("resp", "ctx", None)
    block = P("resp", None)
    return jax.shard_map(
        local,
        mesh=mesh,
        in_specs=(token, token, token, block, block, token, token, P("resp"), P()),
        out_specs=(token, token, token, block, block),
        check_vma=False,
    )
```

```python
import math

import jax
import jax.numpy as jnp
from jax import lax
from jax.experimental import pallas as pl
from jax.experimental.pallas import tpu as pltpu
from jax.sharding import PartitionSpec as P

MESH = pl.DeviceIdType.MESH
HEADS = 8
DIM = 128
SCALE = DIM ** (-0.5)
SCALE2 = SCALE * math.log2(math.e)
FLOOR = -1e30
RING = 8
HALF = RING // 2
GROUP = 16
PB = 64
RB = 128
CHUNK = 256
TOKENS = 128
ROWS = TOKENS * HEADS
VMEM = 48 * 1024 * 1024
F32 = jnp.float32
BF16 = jnp.bfloat16


def level_at(s, idx):
    k = (s + 1) // 2
    odd = lax.rem(s, 2)
    return lax.rem(idx + RING + k - 2 * k * odd, RING)


def body(
    q_hbm, rk_hbm, rv_hbm, pk_hbm, pv_hbm, o_hbm, do_hbm, len_ref, order_hbm,
    dq_ref, rdk_ref, rdv_ref, pdk_ref, pdv_ref,
    order_ref, q_ref, o_ref, do_ref, pkv, rkeys, rvalues, qs, dos, qt, dot, delta, pst, gst, mst, m_run, m_dq, l_run, fac, dqt, dqr, inv_v, inv,
    c1_own, c1_send, c1_recv, c2_send, c2_recv,
    rs_send, rs_recv, ag_recv,
    d_own, d_send, d_recv, d_tot, d_xsend, d_xrecv,
    in_s, inv_s, a_rs, a_cr, a_ss, bk_rs, bk_ss, bv_rs, bv_ss,
    c1_ss, c1_rs, c2_ss, c2_rs, rs_ss, rs_rs, ag_ss, ag_rs,
    d_ss, d_rs, dx_ss, dx_rs, token,
):
    resp = lax.axis_index("resp")
    ctx = lax.axis_index("ctx")
    z, xh, core = resp // 4, lax.rem(resp // 2, 2), lax.rem(resp, 2)
    y, xl = ctx // 2, lax.rem(ctx, 2)
    z_low = resp - z * 4

    def at_z(step, across=False):
        low, c = (z_low + 2 - 4 * xh, ctx + 1 - 2 * xl) if across else (z_low, ctx)
        return (lax.rem(z + RING + step, RING) * 4 + low, c)

    def at_y(step, across=False):
        return (resp, lax.rem(y + RING + step, RING) * 2 + (1 - xl if across else xl))

    other_core = (resp + 1 - 2 * core, ctx)
    mirror = (resp + 2 - 4 * xh, ctx + 1 - 2 * xl)
    x_pair = (resp, ctx + 1 - 2 * xl)

    def at_ctx(step):
        return (resp, lax.rem(ctx + step, GROUP))

    def remote(src, dst, ss, rs, device):
        return pltpu.make_async_remote_copy(
            src_ref=src, dst_ref=dst, send_sem=ss, recv_sem=rs,
            device_id=device, device_id_type=MESH,
        )

    barrier = pltpu.get_barrier_semaphore()
    partners = [other_core, mirror, x_pair]
    partners += [at(step, across) for at in (at_z, at_y) for step in (1, -1) for across in (False, True)]
    for device in partners:
        pl.semaphore_signal(barrier, inc=1, device_id=device, device_id_type=MESH)

    p_rows = pl.ds(pl.multiple_of(resp * PB, PB), PB)
    r_rows = pl.ds(pl.multiple_of(ctx * RB, RB), RB)
    moves = (
        (pk_hbm, pkv.at[p_rows, 0:DIM]), (pv_hbm, pkv.at[p_rows, DIM : 2 * DIM]),
        (rk_hbm, rkeys.at[r_rows]), (rv_hbm, rvalues.at[r_rows]),
        (q_hbm, q_ref), (do_hbm, do_ref), (o_hbm, o_ref), (order_hbm, order_ref),
    )
    reads = [pltpu.make_async_copy(src, dst, in_s.at[i]) for i, (src, dst) in enumerate(moves)]
    for read in reads:
        read.start()
    for read in reads[:4]:
        read.wait()
    pl.semaphore_wait(barrier, len(partners))

    def p_block(lev, sub, c):
        return lev * 4 + sub * 2 + c

    def p_slot(b):
        return pkv.at[pl.ds(pl.multiple_of(b * PB, PB), PB)]

    def r_slot(buffer):
        return lambda b: buffer.at[pl.ds(pl.multiple_of(b * RB, RB), RB)]

    def a_block(s, own):
        return p_block(level_at(s, z), xh if own else 1 - xh, core)

    def b_block(s, own):
        return level_at(s, y) * 2 + (xl if own else 1 - xl)

    ring_a = (p_slot, a_block, lambda b: a_rs.at[b // 2], a_ss, at_z)
    ring_k = (r_slot(rkeys), b_block, lambda b: bk_rs.at[b], bk_ss, at_y)
    ring_v = (r_slot(rvalues), b_block, lambda b: bv_rs.at[b], bv_ss, at_y)

    def ring_copy(ring, s, own, device):
        slot, block, rs, ss, _ = ring
        b = block(s, own)
        return remote(slot(b), slot(b), ss, rs(b), device)

    def arrived(ring, b):
        slot, _, rs, ss, _ = ring
        remote(slot(b), slot(b), ss, rs(b), other_core).wait_recv()

    def core_copy(s, own):
        b = a_block(s, own)
        return remote(p_slot(b), p_slot(b), a_ss, a_cr.at[b // 4], other_core)

    def core_arrived(lev):
        both = pkv.at[pl.ds(pl.multiple_of(lev * CHUNK, CHUNK), 2 * PB)]
        remote(both, both, a_ss, a_cr.at[lev], other_core).wait_recv()

    def all_sent(ref, ss):
        remote(ref, ref, ss, dx_rs.at[0], other_core).wait_send()

    def hops(ring, s, own):
        k = (s + 1) // 2
        odd = lax.rem(s, 2) == 1
        up_limit, down_limit = (HALF, HALF - 1) if own else (HALF - 1, HALF)

        @pl.when(odd & (k < up_limit))
        def _():
            ring_copy(ring, s, own, ring[4](1)).start()

        @pl.when(jnp.logical_not(odd) & (k < down_limit))
        def _():
            ring_copy(ring, s, own, ring[4](-1)).start()

    def ring_step(ring, s, own):
        arrived(ring, ring[1](s, own))
        hops(ring, s, own)
        if ring is ring_a:
            core_copy(s, own).start()

    for across in (False, True):
        for ring in (ring_a, ring_k):
            for step in (1, -1):
                ring_copy(ring, 0, True, ring[4](step, across)).start()
    core_copy(0, True).start()
    ring_copy(ring_a, 0, True, mirror).start()
    ring_copy(ring_k, 0, True, x_pair).start()
    for across in (False, True):
        for step in (1, -1):
            ring_copy(ring_v, 0, True, at_y(step, across)).start()
    ring_copy(ring_v, 0, True, x_pair).start()

    def prepare(h):
        lanes = slice(h * DIM, (h + 1) * DIM)
        q = q_ref[:, lanes]
        do = do_ref[:, lanes]
        qs[lanes, :] = q
        dos[lanes, :] = do
        qt[:, lanes] = q.T
        dot[:, lanes] = do.T
        product = do.astype(F32) * o_ref[:, lanes].astype(F32)
        delta[:, lanes] = jnp.sum(product.T, axis=0, keepdims=True)

    for read in reads[4:]:
        read.wait()
    for h in range(HEADS):
        prepare(h)
    arrived(ring_a, a_block(0, False))
    core_copy(0, False).start()
    arrived(ring_k, b_block(0, False))

    m_run[...] = jnp.full_like(m_run, FLOOR)
    m_dq[...] = jnp.full_like(m_dq, FLOOR)
    l_run[...] = jnp.zeros_like(l_run)
    dqt[...] = jnp.zeros_like(dqt)
    dqr[...] = jnp.zeros_like(dqr)

    places = lax.broadcasted_iota(jnp.int32, (RING * 4, RING * 4), 0)
    stored_at = lax.broadcasted_iota(jnp.int32, (RING * 4, RING * 4), 1)
    found = jnp.max(jnp.where(order_ref[...] == places, stored_at, 0), axis=1, keepdims=True)
    inv_v[:, 0 : RING * 4] = jnp.max(jnp.where(places == stored_at, found, 0), axis=0, keepdims=True)
    inv_copy = pltpu.make_async_copy(inv_v, inv, inv_s)
    inv_copy.start()

    def weights(keys, chunk, key_start):
        s = jnp.dot(keys, qt[...], preferred_element_type=F32) * SCALE2
        if key_start is not None:
            key_pos = key_start + lax.broadcasted_iota(jnp.int32, (CHUNK, ROWS), 0)
            lane = lax.broadcasted_iota(jnp.int32, (CHUNK, ROWS), 1)
            s = jnp.where(key_pos <= ctx * TOKENS + (lane & (TOKENS - 1)), s, FLOOR)
        m_old = m_run[...]
        m_new = jnp.maximum(m_old, jnp.max(s, axis=0, keepdims=True))
        alpha = jnp.exp2(m_old - m_new)
        p = jnp.exp2(s - m_new)
        l_run[...] = l_run[...] * alpha + jnp.sum(p, axis=0, keepdims=True)
        m_run[...] = m_new
        mst[chunk] = m_new
        pst[pl.ds(chunk * 4, 4)] = p.reshape(4, PB, ROWS)
        return p, m_new

    def level_rows(lev):
        return pl.ds(pl.multiple_of(lev * CHUNK, CHUNK), CHUNK)

    def prompt_first(lev):
        keys = pkv[level_rows(lev), 0:DIM]
        p, m_new = weights(keys, lev, None)
        alpha = jnp.exp2(m_dq[...] - m_new)
        m_dq[...] = m_new
        dp = jnp.dot(pkv[level_rows(lev), DIM:], dot[...], preferred_element_type=F32)
        g = p * (dp - delta[...])
        gst[pl.ds(lev * 4, 4)] = g.reshape(4, PB, ROWS)
        dqt[...] = dqt[...] * alpha + jnp.dot(keys.T, g.astype(BF16), preferred_element_type=F32)

    def both_sides(k, then):
        for side in range(2):
            s = 2 * k - 1 + side

            @pl.when((s >= 1) & (s < RING))
            def _():
                then(s)

    def first(k, _):
        for own in (True, False):
            for ring in (ring_a, ring_k):
                both_sides(k + 1, lambda s: ring_step(ring, s, own))

        def prompt_side(s, _):
            @pl.when((s >= 0) & (s < RING))
            def _():
                lev = level_at(s, z)
                core_arrived(lev)
                prompt_first(lev)

            return 0

        lax.fori_loop(2 * k - 1, 2 * k + 1, prompt_side, 0)
        for own in (True, False):
            both_sides(k + 1, lambda s: ring_step(ring_v, s, own))

        def resp_side(s, _):
            lev = level_at(s, y)

            @pl.when((s >= 0) & (s < RING) & (lev <= y))
            def _():
                weights(rkeys[level_rows(lev), :], RING + lev, lev * CHUNK)

            return 0

        lax.fori_loop(2 * k - 1, 2 * k + 1, resp_side, 0)

        return 0

    lax.fori_loop(0, HALF + 1, first, 0)
    arrived(ring_v, b_block(0, False))
    inv_copy.wait()
    pl.semaphore_signal(token, inc=1, device_id=mirror, device_id_type=MESH)

    lane = lax.broadcasted_iota(jnp.int32, (1, ROWS), 1)
    live = ctx * TOKENS + (lane & (TOKENS - 1)) < len_ref[0]
    m_all = m_run[...]
    inv_l = jnp.where(live, 1.0 / l_run[...], 0.0)
    for i in range(2 * RING):
        factor = jnp.exp2(mst[i] - m_all) * inv_l
        for b in range(4):
            fac[4 * i + b] = factor

    def scaled(store, block):
        return (store[block] * fac[block]).astype(BF16)

    def c1_copy(lev):
        return remote(c1_send.at[lev], c1_recv.at[lev], c1_ss, c1_rs.at[lev], other_core)

    def c_term(lev, sub):
        return c1_own[lev, sub] + c1_recv[lev, sub]

    routes = ((4, 2, True, ()), (3, 1, True, ()), (3, 2, False, ()), (2, 2, True, (0, 1)),
              (2, 1, False, ()), (1, 1, True, ()), (1, 1, False, (2, 4)))

    def c_copy(m, up):
        d = 0 if up else 1
        go = routes[m][1]
        return remote(c2_send.at[d, m], c2_recv.at[d, m], c2_ss, c2_rs.at[d, m], at_z(go if up else -go))

    def c_message(m, up):
        d = 0 if up else 1
        dist, _, longer, added = routes[m]
        value = c_term(lax.rem(z + RING + (dist if up else -dist), RING), d if longer else 1 - d)
        for a in added:
            c_copy(a, up).wait_recv()
            value = value + c2_recv[d, a].astype(F32)
        c2_send[d, m] = value.astype(BF16)
        c_copy(m, up).start()

    def c_events(s):
        if s == 6:
            c1_copy(lax.rem(z + HALF, RING)).wait_recv()
            c_message(0, True)
            c_message(0, False)
        plain = {5: (3, True), 4: (3, False), 3: (2, True), 2: (2, False), 1: (1, True), 0: (1, False)}
        if s in plain:
            dist, up = plain[s]
            c1_copy(lax.rem(z + RING + (dist if up else -dist), RING)).wait_recv()
            for m in {3: (1, 2), 2: (4,), 1: (5,)}[dist]:
                c_message(m, up)

    def c_total(sub):
        d = sub
        value = c_term(z, sub)
        for m, up in ((3, d == 0), (5, d == 0), (6, d == 1)):
            value = value + c2_recv[0 if up else 1, m].astype(F32)
        return value

    holds = lax.rem(y, 2) == xl

    def rs_copy(dx, step):
        to_xh = xh if dx == 0 else 1 - xh
        to_y = lax.rem(y + step, RING)
        return remote(
            rs_send.at[to_xh, to_y], rs_recv.at[(dx * RING + step) * 2 + xl], rs_ss, rs_rs,
            (z * 4 + to_xh * 2 + core, 2 * to_y + lax.rem(to_y, 2)),
        )

    def ag_copy(step):
        return remote(ag_recv.at[y], ag_recv.at[y], ag_ss, ag_rs, at_ctx(step))

    far_first = (4, 3, 5, 2, 6, 1, 7, 0)

    def c_scatter():
        c1_copy(z).wait_recv()
        for up in (True, False):
            for m in (3, 5, 6):
                c_copy(m, up).wait_recv()
        for sub in range(2):
            value = c_total(sub).astype(BF16)
            for i in range(RING):
                r, c = i // 2, i % 2
                rs_send[sub, i] = value[r * 16 : (r + 1) * 16, c * DIM : (c + 1) * DIM]
        pl.semaphore_wait(token, 1)
        for step in far_first[:-1]:
            rs_copy(1, step).start()
            rs_copy(0, step).start()
        rs_copy(1, 0).start()

        @pl.when(holds)
        def _():
            rs_recv[xl] = rs_send[xh, y]

        @pl.when(jnp.logical_not(holds))
        def _():
            rs_copy(0, 0).start()

    def c_gather():
        @pl.when(holds)
        def _():
            rest = rs_recv.at[0 : 4 * RING - 1]
            remote(rest, rest, rs_ss, rs_rs, other_core).wait_recv()
            piece = rs_recv[0].astype(F32)
            for i in range(1, 4 * RING):
                piece = piece + rs_recv[i].astype(F32)
            ag_recv[y] = piece.astype(BF16)
            for step in (8, 7, 9, 6, 10, 5, 11, 4, 12, 3, 13, 2, 14, 1, 15):
                ag_copy(step).start()

    def c_finish():
        @pl.when(holds)
        def _():
            rest = ag_recv.at[0 : RING - 1]
            remote(rest, rest, ag_ss, ag_rs, other_core).wait_recv()

        @pl.when(jnp.logical_not(holds))
        def _():
            remote(ag_recv, ag_recv, ag_ss, ag_rs, other_core).wait_recv()

        for c, out in ((0, pdk_ref), (1, pdv_ref)):
            for r in range(RING // 2):
                out[r * 16 : (r + 1) * 16, :] = ag_recv[2 * r + c]

    def d_copy(j, kv, up):
        d = 0 if up else 1
        at = at_y(1 if up else -1)
        if j == 1:
            return remote(d_send.at[d, 0, kv, d], d_recv.at[d, 0, kv, d], d_ss.at[0], d_rs.at[d, 0, kv], at)
        return remote(d_send.at[d, j - 1, kv], d_recv.at[d, j - 1, kv], d_ss.at[1], d_rs.at[d, j - 1, kv], at)

    def d_step(j):
        dist = HALF + 1 - j
        for kv in range(2):
            for up in (True, False):
                d = 0 if up else 1
                if j > 1:
                    d_copy(j - 1, kv, up).wait_recv()
                lev = lax.rem(y + RING + (dist if up else -dist), RING)
                for sub in range(2):
                    begins = sub == d
                    if j == 1 and not begins:
                        continue
                    value = d_own[lev, kv, sub]
                    if j > 2 or (j == 2 and begins):
                        value = value + d_recv[d, j - 2, kv, sub].astype(F32)
                    d_send[d, j - 1, kv, sub] = value.astype(BF16)
                d_copy(j, kv, up).start()

    def resp_level(s):
        lev = level_at(s, y)

        @pl.when(lev <= y)
        def _():
            keys = rkeys[level_rows(lev), :]
            dp = jnp.dot(rvalues[level_rows(lev), :], dot[...], preferred_element_type=F32)
            block = (RING + lev) * 4
            p = pst[pl.ds(block, 4)].reshape(CHUNK, ROWS) * fac[block]
            g = (p * (dp - delta[...])).astype(BF16)
            dv = jnp.dot(p.astype(BF16), dos[...], preferred_element_type=F32)
            dk = jnp.dot(g, qs[...], preferred_element_type=F32) * SCALE
            dqr[...] += jnp.dot(keys.T, g, preferred_element_type=F32)
            for sub in range(2):
                rows = slice(sub * RB, (sub + 1) * RB)
                d_own[lev, 0, sub] = dk[rows]
                d_own[lev, 1, sub] = dv[rows]

        @pl.when(lev > y)
        def _():
            d_own[lev] = jnp.zeros((2, 2, RB, DIM), F32)

    def prompt_second(i, _):
        s = RING - 1 - i
        lev = level_at(s, z)
        ps, gs = [], []
        for b in range(4):
            stored = inv[0, lev * 4 + b]
            ps.append(scaled(pst, stored))
            gs.append(scaled(gst, stored))
        dv = jnp.dot(jnp.concatenate(ps, axis=0), dos[...], preferred_element_type=F32)
        dk = jnp.dot(jnp.concatenate(gs, axis=0), qs[...], preferred_element_type=F32) * SCALE
        for sub in range(2):
            for c in range(2):
                rows = slice((sub * 2 + c) * PB, (sub * 2 + c + 1) * PB)

                @pl.when(core == c)
                def _():
                    c1_own[lev, sub, :, 0:DIM] = dk[rows]
                    c1_own[lev, sub, :, DIM:] = dv[rows]

                @pl.when(core != c)
                def _():
                    c1_send[lev, sub, :, 0:DIM] = dk[rows]
                    c1_send[lev, sub, :, DIM:] = dv[rows]

        c1_copy(lev).start()

        for when in range(RING - 1):

            @pl.when(s == when)
            def _():
                c_events(when)

        @pl.when(s == 5)
        def _():
            resp_level(RING - 1)
            d_step(1)

        return 0

    lax.fori_loop(0, RING, prompt_second, 0)
    c_message(3, True)
    c_message(3, False)

    def resp_second(i, _):
        s = RING - 2 - i
        resp_level(s)

        @pl.when(s == 6)
        def _():
            c_message(6, True)
            c_message(6, False)

        @pl.when(s == 5)
        def _():
            d_step(2)

        @pl.when(s == 3)
        def _():
            c_scatter()

        return 0

    lax.fori_loop(0, RING - 1, resp_second, 0)

    dq_factor = jnp.exp2(m_dq[...] - m_all) * inv_l
    for h in range(HEADS):
        lanes = slice(h * DIM, (h + 1) * DIM)
        dq = dqt[:, lanes] * dq_factor[:, lanes] + dqr[:, lanes]
        dq_ref[:, lanes] = (dq * SCALE).T.astype(BF16)

    d_step(3)

    d_step(4)
    c_gather()

    for kv in range(2):
        for up in (True, False):
            d_copy(HALF, kv, up).wait_recv()
        for sub in range(2):
            d_tot[kv, sub] = d_own[y, kv, sub] + sum(d_recv[d, HALF - 1, kv, sub].astype(F32) for d in range(2))
        d_xsend[kv] = d_tot[kv, 1 - xl].astype(BF16)

    def dx_copy(kv):
        return remote(d_xsend.at[kv], d_xrecv.at[kv], dx_ss, dx_rs.at[kv], x_pair)

    for kv in range(2):
        dx_copy(kv).start()
    for kv, out in ((0, rdk_ref), (1, rdv_ref)):
        dx_copy(kv).wait_recv()
        out[...] = (d_tot[kv, xl] + d_xrecv[kv].astype(F32)).astype(BF16)

    c_finish()

    all_sent(pkv.at[0 : 31 * PB], a_ss)
    all_sent(rkeys.at[0 : 15 * RB], bk_ss)
    all_sent(rvalues.at[0 : 15 * RB], bv_ss)
    all_sent(c1_send, c1_ss)
    all_sent(c2_send, c2_ss)
    all_sent(d_send.at[0, 0], d_ss.at[0])
    all_sent(d_send.at[:, 1:HALF], d_ss.at[1])
    all_sent(d_xsend, dx_ss)

    @pl.when(holds)
    def _():
        all_sent(rs_recv.at[0:15], rs_ss)
        all_sent(rs_recv.at[0:15], ag_ss)

    @pl.when(jnp.logical_not(holds))
    def _():
        all_sent(rs_recv.at[0:16], rs_ss)


def hand_over(*refs):
    n = len(refs) // 2
    for i in range(n):
        refs[n + i][...] = refs[i][...]


def local(query, resp_key, resp_value, prompt_key, prompt_value, saved_out, out_grad, resp_len, prompt_order):
    vmem = pl.BlockSpec(memory_space=pltpu.VMEM)
    smem = pl.BlockSpec(memory_space=pltpu.SMEM)
    dma = pltpu.SemaphoreType.DMA
    wide = 2 * DIM
    outs = pl.pallas_call(
        body,
        out_shape=(
            jax.ShapeDtypeStruct((TOKENS, HEADS * DIM), BF16),
            jax.ShapeDtypeStruct((RB, DIM), BF16),
            jax.ShapeDtypeStruct((RB, DIM), BF16),
            jax.ShapeDtypeStruct((PB, DIM), BF16),
            jax.ShapeDtypeStruct((PB, DIM), BF16),
        ),
        in_specs=[pl.BlockSpec(memory_space=pltpu.HBM)] * 7 + [smem, pl.BlockSpec(memory_space=pltpu.HBM)],
        out_specs=(vmem,) * 5,
        scratch_shapes=[
            pltpu.VMEM((1, RING * 4), jnp.int32),
            pltpu.VMEM((TOKENS, ROWS), BF16),
            pltpu.VMEM((TOKENS, ROWS), BF16),
            pltpu.VMEM((TOKENS, ROWS), BF16),
            pltpu.VMEM((RING * CHUNK, wide), BF16),
            pltpu.VMEM((RING * CHUNK, DIM), BF16),
            pltpu.VMEM((RING * CHUNK, DIM), BF16),
            pltpu.VMEM((ROWS, DIM), BF16),
            pltpu.VMEM((ROWS, DIM), BF16),
            pltpu.VMEM((DIM, ROWS), BF16),
            pltpu.VMEM((DIM, ROWS), BF16),
            pltpu.VMEM((1, ROWS), F32),
            pltpu.VMEM((2 * RING * 4, PB, ROWS), F32),
            pltpu.VMEM((RING * 4, PB, ROWS), F32),
            pltpu.VMEM((2 * RING, 1, ROWS), F32),
            pltpu.VMEM((1, ROWS), F32),
            pltpu.VMEM((1, ROWS), F32),
            pltpu.VMEM((1, ROWS), F32),
            pltpu.VMEM((2 * RING * 4, 1, ROWS), F32),
            pltpu.VMEM((DIM, ROWS), F32),
            pltpu.VMEM((DIM, ROWS), F32),
            pltpu.VMEM((1, DIM), jnp.int32),
            pltpu.SMEM((1, DIM), jnp.int32),
            pltpu.VMEM((RING, 2, PB, wide), F32),
            pltpu.VMEM((RING, 2, PB, wide), F32),
            pltpu.VMEM((RING, 2, PB, wide), F32),
            pltpu.VMEM((2, 7, PB, wide), BF16),
            pltpu.VMEM((2, 7, PB, wide), BF16),
            pltpu.VMEM((2, RING, 16, DIM), BF16),
            pltpu.VMEM((4 * RING, 16, DIM), BF16),
            pltpu.VMEM((RING, 16, DIM), BF16),
            pltpu.VMEM((RING, 2, 2, RB, DIM), F32),
            pltpu.VMEM((2, HALF, 2, 2, RB, DIM), BF16),
            pltpu.VMEM((2, HALF, 2, 2, RB, DIM), BF16),
            pltpu.VMEM((2, 2, RB, DIM), F32),
            pltpu.VMEM((2, RB, DIM), BF16),
            pltpu.VMEM((2, RB, DIM), BF16),
            dma((8,)),
            dma,
            dma((RING * 2,)),
            dma((RING,)),
            dma,
            dma((GROUP,)),
            dma,
            dma((GROUP,)),
            dma,
            dma,
            dma((RING,)),
            dma,
            dma((2, 7)),
            dma,
            dma,
            dma,
            dma,
            dma((2,)),
            dma((2, HALF, 2)),
            dma,
            dma((2,)),
            pltpu.SemaphoreType.REGULAR,
        ],
        compiler_params=pltpu.CompilerParams(
            collective_id=0, has_side_effects=True, vmem_limit_bytes=VMEM
        ),
        name="attention_backward",
    )(
        *(pltpu.with_memory_space_constraint(x, pltpu.HBM) for x in (
            query[0], resp_key[0], resp_value[0], prompt_key, prompt_value, saved_out[0], out_grad[0],
        )),
        resp_len, pltpu.with_memory_space_constraint(prompt_order[None], pltpu.HBM),
    )
    outs = pl.pallas_call(
        hand_over,
        out_shape=tuple(jax.ShapeDtypeStruct(out.shape, out.dtype) for out in outs),
        in_specs=[vmem] * 5,
        out_specs=(vmem,) * 5,
        compiler_params=pltpu.CompilerParams(vmem_limit_bytes=VMEM),
        name="hand_over",
    )(*outs)
    return (outs[0][None], outs[1][None], outs[2][None], outs[3], outs[4])


def solution(mesh):
    token = P("resp", "ctx", None)
    block = P("resp", None)
    return jax.shard_map(
        local,
        mesh=mesh,
        in_specs=(token, token, token, block, block, token, token, P("resp"), P()),
        out_specs=(token, token, token, block, block),
        check_vma=False,
    )
```
